256 devices in a mesh: dp: 32 (over y, x, core), mp: 4 (over z_lo), rep: 2 (over z_hi).
Axes of the slice: x: 4, y: 4, z: 8 (z_hi: 2, z_lo: 4; z = z_hi * 4 + z_lo), core: 2. Of those that a mesh axis runs over, the one named last changes fastest.
Arguments:
- emb_a: bfloat16 [16384, 1024], P(('dp', 'rep'), 'mp'), may hold values from -3 to 3
- emb_b: bfloat16 [16384, 1024], P(('dp', 'rep'), 'mp'), may hold values from -3 to 3
- keep: int32 [16384], P(('dp', 'rep')), may hold values from 0 to 1, as said below
- loss_scale: float32 [1], replicated, may hold values from 4096 to 16384
- hidden_a: bfloat16 [16384, 4096], P(('dp', 'rep')), may hold values from -6 to 6
- proj_a: bfloat16 [4096, 1024], P(('dp', 'rep'), 'mp'), may hold values from -0.09375 to 0.09375
Outputs:
- grad_hidden: bfloat16 [16384, 4096], P(('dp', 'rep'), 'mp')
- grad_proj: float32 [4096, 1024], P(('dp', 'rep'), 'mp')
- grad_emb_b: bfloat16 [16384, 1024], P(('dp', 'rep'), 'mp')
The draws below stay inside these ranges and needn't reach their ends.
Inputs may be any that keep to these rules, and one draw needn't show every extreme that they name: `keep`: the pair at every index divisible by 64 is kept.
All inputs are finite; a program needn't handle non-finite values.
Results may differ from the reference program's by a relative error of at most 0.0074.
Values may be sent and summed in bfloat16 or wider, within the bound.
No kernel may reach another device: no remote copies, remote signals or barrier semaphores. Data moves between devices by JAX's collectives and lax.ppermute only.
A program may use at most 128 MiB of HBM per device.

```python
import math
import jax
import jax.numpy as jnp
from jax import lax

EMBED = 1024
PROJ_IN = 4096
PAIRS = 16384


def base_rows(key):
    normal = jnp.clip(jax.random.normal(jax.random.fold_in(key, 1), (PAIRS, EMBED), jnp.float32), -5.0, 5.0)
    return normal


def row_scales(key):
    return jnp.exp(jax.random.uniform(key, (PAIRS, 1), jnp.float32, math.log(0.05), math.log(0.5)))


def draw_emb_a(key, part):
    own_key = jax.random.fold_in(key, 3)
    shared = base_rows(key)
    direction = shared
    return (row_scales(jax.random.fold_in(own_key, 5)) * direction).astype(jnp.bfloat16)


def draw_emb_b(key, part):
    own_key = jax.random.fold_in(key, 4)
    shared = base_rows(key)
    noise = base_rows(jax.random.fold_in(own_key, 1))
    direction = 0.15 * shared + noise
    return (row_scales(jax.random.fold_in(own_key, 2)) * direction).astype(jnp.bfloat16)


def draw_keep(key, part):
    key = jax.random.fold_in(key, 5)
    position = jnp.arange(PAIRS, dtype=jnp.int32)
    level = 150 + 800 * position // PAIRS
    values = jax.random.randint(key, (PAIRS,), 0, 1000, dtype=jnp.int32)
    return jnp.where((values < level) | (position % 64 == 0), 1, 0).astype(jnp.int32)


def shard_levels(key, dims, cuts, smallest, largest):
    def one(axis_at, shards_of):
        heights = jax.random.uniform(jax.random.fold_in(jax.random.fold_in(key, 6), axis_at), (shards_of,), jnp.float32, smallest / len(cuts), largest / len(cuts))
        return jnp.repeat(jnp.exp(heights), dims[axis_at] // shards_of).reshape((-1,) + (1,) * (len(dims) - axis_at - 1))

    gain = one(*cuts[0])
    for cut in cuts[1:]:
        gain = gain * one(*cut)
    return gain


def centred(stream_key, shape, width, bound, shards=(), held_as=jnp.bfloat16):
    loudness = shard_levels(stream_key, shape, shards, -0.22, 0.18) if shards else 1.0
    entries = jax.random.normal(stream_key, shape, jnp.float32) * width * loudness
    return jnp.minimum(jnp.maximum(entries, -bound), bound).astype(held_as)


def setup_inputs(seed: int = 0) -> dict:
    key_list = jax.random.split(jax.random.key(seed), 7)
    emb_a = draw_emb_a(jax.random.fold_in(key_list[6], 71), 0)
    emb_b = draw_emb_b(jax.random.fold_in(key_list[6], 71), 0)
    keep = draw_keep(jax.random.fold_in(key_list[6], 71), 0)
    loss_scale = jnp.clip(jnp.exp(jax.random.uniform(key_list[3], (1,), jnp.float32, math.log(4096.0), math.log(16384.0))), 4096.0, 16384.0)
    hidden_a = centred(key_list[4], (PAIRS, PROJ_IN), 1.0, 6.0, ((0, 64),))
    proj_a = centred(key_list[5], (PROJ_IN, EMBED), PROJ_IN ** -0.5, 0.09375, ((0, 64), (1, 4)))
    return dict(emb_a=emb_a, emb_b=emb_b, keep=keep, loss_scale=loss_scale, hidden_a=hidden_a, proj_a=proj_a)


logit_scale = 100.0
masked_score = -1e+30
epsilon = 1e-06

def normalize(wide):
    values = wide.astype(jnp.float32)
    norms = jnp.sqrt(lax.optimization_barrier(jnp.sum(values * values, axis=-1)) + epsilon)
    return (norms, (values / norms[..., None]).astype(jnp.bfloat16))

def unit_backward(grads, wide, norms):
    values = wide.astype(jnp.float32)
    unit = values / norms[..., None]
    dots = lax.optimization_barrier(jnp.sum(unit * grads, axis=-1))
    return (grads - unit * dots[..., None]) / norms[..., None]

def tile_weights(scores, row_keep, col_keep, row_lse, col_lse, diagonal):
    kept_rows = row_keep.astype(jnp.float32)
    kept_cols = col_keep.astype(jnp.float32)
    masked_cols = jnp.where(kept_cols[None, :] > 0, scores, masked_score)
    masked_rows = jnp.where(kept_rows[:, None] > 0, scores, masked_score)
    first = jnp.exp(masked_cols - row_lse[:, None])
    second = jnp.exp(masked_rows - col_lse[None, :])
    mixed = kept_rows[:, None] * kept_cols[None, :] * (first + second)
    return (mixed - 2.0 * jnp.where(diagonal, kept_rows[:, None], 0.0)).astype(jnp.bfloat16)

def reference(emb_a, emb_b, keep, loss_scale, hidden_a, proj_a):
    norm_a, unit_a = normalize(emb_a)
    norm_b, unit_b = normalize(emb_b)
    kept = keep.astype(jnp.float32)
    count = jnp.sum(kept)
    coef = loss_scale[0] * logit_scale / (2.0 * count)
    block = math.gcd(PAIRS, 1024)
    starts = jnp.arange(PAIRS // block, dtype=jnp.int32) * block
    units_a32 = unit_a.astype(jnp.float32)
    units_b32 = unit_b.astype(jnp.float32)
    all_ids = jnp.arange(PAIRS, dtype=jnp.int32)

    def scores_at(start):
        rows = lax.dynamic_slice_in_dim(units_a32, start, block, 0)
        return (rows, logit_scale * jnp.dot(rows, units_b32.T, precision=lax.Precision.HIGHEST))

    def first_pass(carry, start):
        col_top, col_total = carry
        rows, scores = scores_at(start)
        row_keep = lax.dynamic_slice_in_dim(kept, start, block, 0)
        masked_cols = jnp.where(kept[None, :] > 0, scores, masked_score)
        top = lax.optimization_barrier(jnp.max(masked_cols, axis=1))
        row_lse = top + jnp.log(lax.optimization_barrier(jnp.sum(jnp.exp(masked_cols - top[:, None]), axis=1)))
        masked_rows = jnp.where(row_keep[:, None] > 0, scores, masked_score)
        new_top = jnp.maximum(col_top, lax.optimization_barrier(jnp.max(masked_rows, axis=0)))
        col_total = col_total * jnp.exp(col_top - new_top) + lax.optimization_barrier(jnp.sum(jnp.exp(masked_rows - new_top[None, :]), axis=0))
        return ((new_top, col_total), row_lse)
    start_carry = (jnp.full((PAIRS,), masked_score, jnp.float32), jnp.zeros((PAIRS,), jnp.float32))
    (col_top, col_total), row_lse = lax.scan(first_pass, start_carry, starts)
    row_lse = row_lse.reshape(PAIRS)
    col_lse = col_top + jnp.log(col_total)

    def second_pass(grad_b, start):
        rows, scores = scores_at(start)
        row_keep = lax.dynamic_slice_in_dim(kept, start, block, 0)
        lse_block = lax.dynamic_slice_in_dim(row_lse, start, block, 0)
        row_ids = start + jnp.arange(block, dtype=jnp.int32)
        diagonal = row_ids[:, None] == all_ids[None, :]
        weights = tile_weights(scores, row_keep, kept, lse_block, col_lse, diagonal).astype(jnp.float32)
        grad_a = coef * jnp.dot(weights, units_b32, precision=lax.Precision.HIGHEST)
        grad_b = grad_b + coef * jnp.dot(weights.T, rows, precision=lax.Precision.HIGHEST)
        return (grad_b, grad_a)
    grad_b, grad_a = lax.scan(second_pass, jnp.zeros((PAIRS, EMBED), jnp.float32), starts)
    grad_a = grad_a.reshape(PAIRS, EMBED)
    grad_emb_a = unit_backward(grad_a, emb_a, norm_a).astype(jnp.bfloat16)
    grad_emb_b = unit_backward(grad_b, emb_b, norm_b).astype(jnp.bfloat16)
    grad_proj = jnp.dot(hidden_a.T, grad_emb_a, preferred_element_type=jnp.float32)
    grad_hidden = jnp.dot(grad_emb_a, proj_a.T, preferred_element_type=jnp.float32).astype(jnp.bfloat16)
    return (grad_hidden, grad_proj, grad_emb_b)
```

```python
import jax
import jax.numpy as jnp
from jax import lax
from jax.experimental import pallas as pl
from jax.experimental.pallas import tpu as pltpu
from jax.sharding import PartitionSpec as P

logit_scale = 100.0
masked_score = -1e30
epsilon = 1e-06
NX, NY, NC = 4, 4, 2
NM, NR = 4, 2
NZ = NM * NR
bf16 = jnp.bfloat16
f32 = jnp.float32


def dp_index(y, x, c):
    return ((y % NY) * NX + x % NX) * NC + c % NC


def dp_perm(to):
    return [
        (dp_index(y, x, c), dp_index(*to(y, x, c)))
        for y in range(NY)
        for x in range(NX)
        for c in range(NC)
    ]


def z_index(z):
    z = z % NZ
    return (z % NM) * NR + z // NM


def from_x(v, d):
    return lax.ppermute(v, "dp", dp_perm(lambda y, x, c: (y, x - d, c)))


def from_y(v, d):
    return lax.ppermute(v, "dp", dp_perm(lambda y, x, c: (y - d, x, c)))


def from_core(v):
    return lax.ppermute(v, "dp", dp_perm(lambda y, x, c: (y, x, 1 - c)))


def from_dp_xor(v, k):
    return lax.ppermute(v, "dp", [(i, i ^ k) for i in range(NX * NY * NC)])


def from_z(v, d):
    return lax.ppermute(v, ("mp", "rep"), [(z_index(z), z_index(z - d)) for z in range(NZ)])


def from_z_xor(v, k):
    return lax.ppermute(v, ("mp", "rep"), [(z_index(z), z_index(z ^ k)) for z in range(NZ)])


def from_mp(v, d):
    return lax.ppermute(v, "mp", [(m, (m - d) % NM) for m in range(NM)])


def from_rep(v):
    return lax.ppermute(v, "rep", [(0, 1), (1, 0)])


OFFSETS = (0, 1, 2, -1)
Z_OFFSETS = (0, 1, 2, 3, 4, -3, -2, -1)


def plane_gather(piece):
    half = piece.shape[0] // 2
    first, second = piece[:half], piece[half:]
    wide_0 = [first] + [None] * 3
    wide_1 = [second] + [None] * 3
    for i in (1, 2, 3):
        wide_0[i] = from_x(first, OFFSETS[i])
        wide_1[i] = from_y(second, OFFSETS[i])
    wide_0, wide_1 = jnp.concatenate(wide_0, 0), jnp.concatenate(wide_1, 0)
    full_0 = [wide_0] + [None] * 3
    full_1 = [wide_1] + [None] * 3
    for i in (1, 2, 3):
        full_0[i] = from_y(wide_0, OFFSETS[i])
        full_1[i] = from_x(wide_1, OFFSETS[i])
    return jnp.concatenate(full_0 + full_1, 0)


def plane_sum(first, second):
    part = first.shape[0] // 4
    got_0, got_1 = [], []
    for i in (1, 2, 3):
        got_0.append(from_y(first[i * part : (i + 1) * part], -OFFSETS[i]))
        got_1.append(from_x(second[i * part : (i + 1) * part], -OFFSETS[i]))
    sum_0 = sum([g.astype(f32) for g in got_0], first[:part].astype(f32))
    sum_1 = sum([g.astype(f32) for g in got_1], second[:part].astype(f32))
    low_0, low_1 = sum_0.astype(bf16), sum_1.astype(bf16)
    piece = part // 4
    got_0, got_1 = [], []
    for i in (1, 2, 3):
        got_0.append(from_x(low_0[i * piece : (i + 1) * piece], -OFFSETS[i]))
        got_1.append(from_y(low_1[i * piece : (i + 1) * piece], -OFFSETS[i]))
    out_0 = sum([g.astype(f32) for g in got_0], sum_0[:piece])
    out_1 = sum([g.astype(f32) for g in got_1], sum_1[:piece])
    return jnp.concatenate([out_0, out_1], 0)


def z_gather(piece):
    return jnp.concatenate([piece] + [from_z(piece, d) for d in Z_OFFSETS[1:]], 0)


def z_sum(parts):
    rows = parts.shape[0] // NZ
    low = parts.astype(bf16)
    got = [
        from_z(low[(i + 1) * rows : (i + 2) * rows], -d) for i, d in enumerate(Z_OFFSETS[1:])
    ]
    return sum([g.astype(f32) for g in got], parts[:rows])


def turned(blocks, shift, axis):
    n = len(blocks)
    size = blocks[0].shape[axis]
    doubled = jnp.concatenate(list(blocks) + list(blocks)[:-1], axis)
    return lax.dynamic_slice_in_dim(doubled, shift % n * size, n * size, axis)


def block_at(v, index, axis, n):
    size = v.shape[axis] // n
    return lax.dynamic_slice_in_dim(v, index % n * size, size, axis)


def rows_aligned(v, along, d):
    n = v.shape[0] // 2
    first, second = v[:n].reshape(NY, NX, -1), v[n:].reshape(NX, NY, -1)
    first = jnp.roll(first, d, 1 if along == "x" else 0)
    second = jnp.roll(second, d, 0 if along == "x" else 1)
    return jnp.concatenate([first.reshape(n), second.reshape(n)])


def cols_aligned(v, d):
    n = 128 * (v.shape[0] // 128 - 1)
    cols, tail = v[:n].reshape(NC, NZ, -1), v[n:]
    cols = jnp.roll(cols, d, 1) if d else cols[::-1]
    return jnp.concatenate([cols.reshape(n), tail])


def log_add(a, b):
    return jnp.maximum(a, b) + jnp.log1p(jnp.exp(-jnp.abs(a - b)))


def unit_backward(grads, wide, norms):
    unit = wide / norms[..., None]
    dots = jnp.sum(unit * grads, axis=-1)
    return (grads - unit * dots[..., None]) / norms[..., None]


def hidden_prepared(hidden, y_at, x_at, c_at, mp_at):
    rows, width = hidden.shape
    wide = width // (NX * NY * NC)
    half = wide // 2

    def kernel(at, hidden_ref, out_ref, turned_ref):
        piece = rows // NM
        for k in range(NM):
            source = lax.rem(at[3] + NM - k, NM)
            turned_ref[k * piece : (k + 1) * piece, :] = hidden_ref[
                pl.ds(pl.multiple_of(source * piece, piece), piece), :
            ]
        for c in range(NC):
            for i, dy in enumerate(OFFSETS):
                for j, dx in enumerate(OFFSETS):
                    y = lax.rem(at[0] + NY + dy, NY)
                    x = lax.rem(at[1] + NX + dx, NX)
                    core = lax.rem(at[2] + c, NC)
                    column = ((y * NX + x) * NC + core) * wide
                    block = turned_ref[:, pl.ds(pl.multiple_of(column, wide), wide)]
                    block = block.astype(f32).T.astype(bf16)
                    out_ref[c, 0, i * NX + j] = block[:half]
                    out_ref[c, 1, j * NY + i] = block[half:]

    return pl.pallas_call(
        kernel,
        out_shape=jax.ShapeDtypeStruct((NC, 2, NX * NY, half, rows), bf16),
        in_specs=[
            pl.BlockSpec(memory_space=pltpu.SMEM),
            pl.BlockSpec(memory_space=pltpu.VMEM),
        ],
        out_specs=pl.BlockSpec(memory_space=pltpu.VMEM),
        scratch_shapes=[pltpu.VMEM((rows, width), bf16)],
        compiler_params=pltpu.CompilerParams(vmem_limit_bytes=24 * 2**20),
    )(jnp.stack([y_at, x_at, c_at, mp_at]).astype(jnp.int32), hidden)


def gather_proj(proj, y_at, x_at, c_at, mp_at, rep_at):
    rows, feats = proj.shape
    z_at = rep_at * NM + mp_at
    got = {d % NZ: (from_z(proj, d) if d else proj) for d in Z_OFFSETS}
    ring = turned([got[d] for d in range(NZ)], NZ - z_at, 0)
    wide = ring.reshape(NR, NM, rows, feats).transpose(0, 2, 1, 3).reshape(NR * rows, NM * feats)
    out = jnp.where(y_at == mp_at, wide, jnp.zeros_like(wide))
    for d in (1, 2, 3):
        pairs = [
            (dp_index(m, x, c) * NM + m, dp_index(m + d, x, c) * NM + m)
            for m in range(NM)
            for x in range(NX)
            for c in range(NC)
        ]
        out = out + lax.ppermute(wide, ("dp", "mp"), pairs)
    xs = {d % NX: (from_x(out, d) if d else out) for d in OFFSETS}
    ordered = turned([xs[d] for d in range(NX)], NX - x_at, 0)
    other = from_core(ordered)
    mine_first = c_at == 0
    low = jnp.where(mine_first, ordered, other).reshape(NX, NR * rows, NM * feats)
    high = jnp.where(mine_first, other, ordered).reshape(NX, NR * rows, NM * feats)
    return jnp.stack([low, high], 1).reshape(NX * NC * NR * rows, NM * feats)


def body(emb_a, emb_b, keep, loss_scale, hidden_a, proj_a):
    dp_at = lax.axis_index("dp")
    mp_at = lax.axis_index("mp")
    rep_at = lax.axis_index("rep")
    y_at, x_at, c_at = dp_at // (NX * NC), dp_at // NC % NX, dp_at % NC
    local = emb_a.shape[0]
    piece = local // NM

    both = jnp.stack([emb_a, emb_b])
    parts = [block_at(both, mp_at, 1, NM)]
    for k in (1, 2, 3):
        parts.append(from_mp(block_at(both, mp_at + NM - k, 1, NM), k))
    wide = turned(parts, NM - mp_at, 2).astype(f32)
    norms = jnp.sqrt(jnp.sum(wide * wide, axis=-1) + epsilon)
    units = (wide / norms[..., None]).astype(bf16)
    kept = block_at(keep, mp_at, 0, NM) > 0
    marker = jnp.where(jnp.arange(wide.shape[-1]) == 0, 2.0, 0.0).astype(bf16)
    marked = jnp.where(kept[None, :, None], units, marker[None, None, :])

    rows_u = plane_gather(marked[0])
    cols_own = z_gather(marked[1])
    cols_u = jnp.concatenate([cols_own, from_core(cols_own)], 0)
    kept_rows = rows_u[:, 0] < 1.5
    kept_cols = cols_u[:, 0] < 1.5

    scores = logit_scale * lax.dot_general(
        rows_u, cols_u, (((1,), (1,)), ((), ())), preferred_element_type=f32
    )
    by_cols = jnp.where(kept_cols[None, :], scores, masked_score)
    by_rows = jnp.where(kept_rows[:, None], scores, masked_score)
    row_top = jnp.max(by_cols, 1)
    col_top = jnp.max(by_rows, 0)
    row_lse = row_top + jnp.log(jnp.sum(jnp.exp(by_cols - row_top[:, None]), 1))
    col_lse = col_top + jnp.log(jnp.sum(jnp.exp(by_rows - col_top[None, :]), 0))
    log_count = jnp.log(jnp.sum(kept_rows.astype(f32)))
    col_info = jnp.concatenate([col_lse, jnp.full((128,), log_count, f32)])
    for row_step, col_step in ((("x", 1), 1), (("x", 2), 2), (("y", 1), 4), (("y", 2), 0)):
        along, d = row_step
        row_other = (from_x if along == "x" else from_y)(row_lse, d)
        col_other = from_z(col_info, col_step) if col_step else from_core(col_info)
        row_lse = log_add(row_lse, rows_aligned(row_other, along, d))
        col_info = log_add(col_info, cols_aligned(col_other, col_step))
    col_lse = col_info[: col_lse.shape[0]]
    count = jnp.exp(col_info[col_lse.shape[0]])
    coef = loss_scale[0] * logit_scale / (2.0 * count)

    tile_rows, tile_cols = scores.shape
    half = piece // 2
    row_place = jnp.arange(tile_rows, dtype=jnp.int32)
    col_place = jnp.arange(tile_cols, dtype=jnp.int32)
    second = row_place >= tile_rows // 2
    partner = jnp.where(second, row_place - tile_rows // 2 + half, row_place)
    limit = jnp.where(second, 2 * half, half)
    partner = jnp.where(partner < limit, partner, -1)
    diagonal = partner[:, None] == col_place[None, :]
    keep_both = kept_rows[:, None] & kept_cols[None, :]
    mixed = jnp.where(
        keep_both,
        jnp.exp(by_cols - row_lse[:, None]) + jnp.exp(by_rows - col_lse[None, :]),
        0.0,
    )
    weights = (mixed - jnp.where(diagonal & kept_rows[:, None], 2.0, 0.0)).astype(bf16)

    row_grads = lax.dot_general(
        weights, cols_u, (((1,), (0,)), ((), ())), preferred_element_type=f32
    ).astype(bf16)
    col_grads = lax.dot_general(
        weights, rows_u, (((0,), (0,)), ((), ())), preferred_element_type=f32
    )
    grads_a = coef * plane_sum(row_grads[: tile_rows // 2], row_grads[tile_rows // 2 :])
    grad_a = unit_backward(grads_a, wide[0], norms[0]).astype(bf16)

    col_low = col_grads[tile_cols // 2 :].astype(bf16)
    grads_b = coef * z_sum(col_grads[: tile_cols // 2] + from_core(col_low).astype(f32))
    grad_b = unit_backward(grads_b, wide[1], norms[1]).astype(bf16)
    got = [block_at(grad_b, mp_at, 1, NM)]
    for k in (1, 2, 3):
        got.append(from_mp(block_at(grad_b, mp_at + NM - k, 1, NM), k))
    grad_emb_b = turned(got, NM - mp_at, 0)

    mine = [block_at(grad_a, mp_at, 1, NM)]
    for k in (1, 2, 3):
        mine.append(from_mp(block_at(grad_a, mp_at + k, 1, NM), -k))
    mine = jnp.concatenate(mine, 0)
    hidden_t = hidden_prepared(hidden_a, y_at, x_at, c_at, mp_at)
    n_out = NX * NY * NC * NR * proj_a.shape[0]
    proj_part = jnp.dot(
        hidden_t.reshape(n_out, local), mine, preferred_element_type=f32
    ).reshape(NC, n_out // NC, -1)
    chip_part = proj_part[0] + from_core(proj_part[1].astype(bf16)).astype(f32)
    chip_part = chip_part.astype(bf16)
    n_half = chip_part.shape[0] // 2
    both_reps = plane_sum(chip_part[:n_half], chip_part[n_half:])
    grad_proj = block_at(both_reps, rep_at, 0, NR) + from_rep(
        block_at(both_reps, 1 - rep_at, 0, NR)
    )

    rows_a = [grad_a] + [from_mp(grad_a, k) for k in (1, 2, 3)]
    rows_a = turned(rows_a, NM - mp_at, 0)
    proj_rows = gather_proj(proj_a, y_at, x_at, c_at, mp_at, rep_at)
    grad_hidden = lax.dot_general(
        rows_a, proj_rows, (((1,), (1,)), ((), ())), preferred_element_type=f32
    ).astype(bf16)
    return (grad_hidden, grad_proj, grad_emb_b)


def solution(mesh):
    return jax.shard_map(
        body,
        mesh=mesh,
        in_specs=(
            P(("dp", "rep"), "mp"),
            P(("dp", "rep"), "mp"),
            P(("dp", "rep")),
            P(),
            P(("dp", "rep"), None),
            P(("dp", "rep"), "mp"),
        ),
        out_specs=(P(("dp", "rep"), "mp"), P(("dp", "rep"), "mp"), P(("dp", "rep"), "mp")),
        check_vma=False,
    )
```

```python
import jax
import jax.numpy as jnp
from jax import lax
from jax.experimental import pallas as pl
from jax.experimental.pallas import tpu as pltpu
from jax.sharding import PartitionSpec as P

logit_scale = 100.0
masked_score = -1e30
epsilon = 1e-06
NX, NY, NC = 4, 4, 2
NM, NR = 4, 2
NZ = NM * NR
bf16 = jnp.bfloat16
f32 = jnp.float32


def dp_index(y, x, c):
    return ((y % NY) * NX + x % NX) * NC + c % NC


def dp_perm(to):
    return [
        (dp_index(y, x, c), dp_index(*to(y, x, c)))
        for y in range(NY)
        for x in range(NX)
        for c in range(NC)
    ]


def z_index(z):
    z = z % NZ
    return (z % NM) * NR + z // NM


def shift_perm(d, swapped):
    return dp_perm(
        lambda y, x, c: (y, x - d, c) if (c == 0) != swapped else (y - d, x, c)
    )


def from_first(v, d):
    return lax.ppermute(v, "dp", shift_perm(d, False))


def from_second(v, d):
    return lax.ppermute(v, "dp", shift_perm(d, True))


def from_x(v, d):
    return lax.ppermute(v, "dp", dp_perm(lambda y, x, c: (y, x - d, c)))


def from_core(v):
    return lax.ppermute(v, "dp", dp_perm(lambda y, x, c: (y, x, 1 - c)))


def from_z(v, d):
    return lax.ppermute(v, ("mp", "rep"), [(z_index(z), z_index(z - d)) for z in range(NZ)])


def from_mp(v, d):
    return lax.ppermute(v, "mp", [(m, (m - d) % NM) for m in range(NM)])


OFFSETS = (0, 1, 2, -1)


def tied(value, *others):
    return lax.optimization_barrier((value, others))[0]


def line_gather(piece):
    return jnp.concatenate([piece] + [from_first(piece, d) for d in OFFSETS[1:]], 0)


def line_sum(blocks):
    got = [from_second(blocks[i], -OFFSETS[i]) for i in (1, 2, 3)]
    return sum([g.astype(f32) for g in got], blocks[0].astype(f32))


def piece_sum(line, low):
    size = low.shape[0] // 4
    got = [from_first(low[i * size : (i + 1) * size], -OFFSETS[i]) for i in (1, 2, 3)]
    return sum([g.astype(f32) for g in got], line[:size])


def turned(blocks, shift, axis):
    n = len(blocks)
    size = blocks[0].shape[axis]
    doubled = jnp.concatenate(list(blocks) + list(blocks)[:-1], axis)
    return lax.dynamic_slice_in_dim(doubled, shift % n * size, n * size, axis)


def block_at(v, index, axis, n):
    size = v.shape[axis] // n
    return lax.dynamic_slice_in_dim(v, index % n * size, size, axis)


def rows_aligned(v, axis, d):
    return jnp.roll(v.reshape(4, 4, -1), d, axis).reshape(v.shape)


def cols_swapped(v):
    n = 128 * (v.shape[0] // 128 - 1) // 2
    return jnp.concatenate([v[n : 2 * n], v[:n], v[2 * n :]])


def log_add(a, b):
    return jnp.maximum(a, b) + jnp.log1p(jnp.exp(-jnp.abs(a - b)))


def normalize(wide):
    norms = jnp.sqrt(jnp.sum(wide * wide, axis=-1) + epsilon)
    return norms, (wide / norms[..., None]).astype(bf16)


def unit_backward(grads, wide, norms):
    unit = wide / norms[..., None]
    dots = jnp.sum(unit * grads, axis=-1)
    return (grads - unit * dots[..., None]) / norms[..., None]


def hidden_prepared(hidden, y_at, x_at, c_at, mp_at):
    rows, width = hidden.shape
    wide = width // (NX * NY * NC)
    half = wide // NR

    def kernel(at, hidden_ref, out_ref, turned_ref):
        piece = rows // NM
        core = at[2]
        for k in range(NM):
            source = lax.rem(at[3] + NM - k, NM)
            turned_ref[k * piece : (k + 1) * piece, :] = hidden_ref[
                pl.ds(pl.multiple_of(source * piece, piece), piece), :
            ]
        for i, dy in enumerate(OFFSETS):
            for j, dx in enumerate(OFFSETS):
                y = lax.rem(at[0] + NY + dy, NY)
                x = lax.rem(at[1] + NX + dx, NX)
                for c in range(NC):
                    column = ((y * NX + x) * NC + c) * wide
                    block = turned_ref[:, pl.ds(pl.multiple_of(column, wide), wide)]
                    block = block.astype(f32).T.astype(bf16)
                    for r in range(NR):
                        place = i * NX + j if r == 0 else j * NY + i
                        slot = lax.rem(core + r, NR)
                        out_ref[slot, place, c] = block[r * half : (r + 1) * half]

    return pl.pallas_call(
        kernel,
        out_shape=jax.ShapeDtypeStruct((NR, NX * NY, NC, half, rows), bf16),
        in_specs=[
            pl.BlockSpec(memory_space=pltpu.SMEM),
            pl.BlockSpec(memory_space=pltpu.VMEM),
        ],
        out_specs=pl.BlockSpec(memory_space=pltpu.VMEM),
        scratch_shapes=[pltpu.VMEM((rows, width), bf16)],
        compiler_params=pltpu.CompilerParams(vmem_limit_bytes=24 * 2**20),
    )(jnp.stack([y_at, x_at, c_at, mp_at]).astype(jnp.int32), hidden)


def call(kernel, out_shape, args, smem=0, scratch=(), vmem=48, cost=None):
    specs = [pl.BlockSpec(memory_space=pltpu.SMEM)] * smem
    specs += [pl.BlockSpec(memory_space=pltpu.VMEM)] * (len(args) - smem)
    return pl.pallas_call(
        kernel,
        out_shape=out_shape,
        in_specs=specs,
        out_specs=jax.tree.map(lambda _: pl.BlockSpec(memory_space=pltpu.VMEM), out_shape),
        scratch_shapes=list(scratch),
        cost_estimate=cost,
        compiler_params=pltpu.CompilerParams(vmem_limit_bytes=vmem * 2**20),
    )(*args)


def shaped(shape, dtype):
    return jax.ShapeDtypeStruct(shape, dtype)


def structure_units(blocks, local):
    _, height, feats = blocks.shape
    extra = height - local

    def kernel(held, units, raw, proj):
        for r in range(NR):
            rows = slice(r * local, (r + 1) * local)
            wide = [held[r * NM + m, :local].astype(f32) for m in range(NM)]
            squares = sum(jnp.sum(w * w, 1, keepdims=True) for w in wide)
            inverse = 1.0 / jnp.sqrt(squares + epsilon)
            dropped = wide[0][:, :1] > 4.0
            lane = lax.broadcasted_iota(jnp.int32, (local, feats), 1)
            for m in range(NM):
                cols = slice(m * feats, (m + 1) * feats)
                marker = jnp.where(lane == 0, 2.0, 0.0) if m == 0 else jnp.zeros_like(wide[m])
                units[rows, cols] = jnp.where(dropped, marker, wide[m] * inverse).astype(bf16)
                raw[rows, cols] = held[r * NM + m, :local]
                proj[r * extra : (r + 1) * extra, cols] = held[r * NM + m, local:]

    out = (
        shaped((NR * local, NM * feats), bf16),
        shaped((NR * local, NM * feats), bf16),
        shaped((NR * extra, NM * feats), bf16),
    )
    return call(kernel, out, [blocks])


def masked_scores(rows, cols):
    part, width = rows[0].shape
    n_rows, n_cols = len(rows) * part, sum(c.shape[0] for c in cols)

    def kernel(*refs):
        row_refs, col_refs = refs[: len(rows)], refs[len(rows) : len(rows) + len(cols)]
        scores, row_out, col_out = refs[len(rows) + len(cols) :]
        first = (lax.broadcasted_iota(jnp.int32, (16, width), 1) == 0).astype(f32).astype(bf16)
        nt = (((1,), (1,)), ((), ()))
        kept_cols = jnp.concatenate(
            [lax.dot_general(first, c[...], nt, preferred_element_type=f32)[:1] for c in col_refs],
            1,
        )
        kept_cols = kept_cols < 1.5
        col_top = None
        count = jnp.zeros((1, 1), f32)
        for t, row in enumerate(row_refs):
            kept_rows = row[:, :1].astype(f32) < 1.5
            count = count + jnp.sum(kept_rows.astype(f32), 0, keepdims=True)
            s = jnp.concatenate(
                [
                    lax.dot_general(row[...], c[...], nt, preferred_element_type=f32)
                    for c in col_refs
                ],
                1,
            )
            s = jnp.where(kept_rows & kept_cols, logit_scale * s, masked_score)
            scores[t] = s
            top = jnp.max(s, 1, keepdims=True)
            lse = top + jnp.log(jnp.sum(jnp.exp(s - top), 1, keepdims=True))
            row_out[:, t * part : (t + 1) * part] = jnp.broadcast_to(lse, (part, 128)).T[:1]
            here = jnp.max(s, 0, keepdims=True)
            col_top = here if col_top is None else jnp.maximum(col_top, here)
        total = jnp.zeros_like(col_top)
        for t in range(len(rows)):
            total = total + jnp.sum(jnp.exp(scores[t] - col_top), 0, keepdims=True)
        col_out[:, :n_cols] = col_top + jnp.log(total)
        col_out[:, n_cols:] = jnp.broadcast_to(jnp.log(count), (1, 128))

    out = (
        shaped((len(rows), part, n_cols), f32),
        shaped((1, n_rows), f32),
        shaped((1, n_cols + 128), f32),
    )
    cost = pl.CostEstimate(
        flops=2 * n_rows * n_cols * width, bytes_accessed=8 * n_rows * n_cols, transcendentals=0
    )
    return call(kernel, out, list(rows) + list(cols), cost=cost)


def weights_and_row_grads(scores, row_lse, col_lse, cols, start, half):
    n_parts, part, n_cols = scores.shape
    width = cols[0].shape[1]
    n_core = n_cols // NC

    def kernel(at, scores_ref, row_ref, col_ref, own, other, weights, *grads):
        col = jnp.maximum(col_ref[:, :n_cols], 0.1 * masked_score)
        for t in range(n_parts):
            row = row_ref[:, t * part : (t + 1) * part]
            row = jnp.broadcast_to(row, (128, part)).T[:, :1]
            row = jnp.maximum(row, 0.1 * masked_score)
            s = scores_ref[t]
            w = jnp.exp(s - row) + jnp.exp(s - col)
            if t == 0:
                n = NC * half
                r = lax.broadcasted_iota(jnp.int32, (n, n_cols), 0)
                c = lax.broadcasted_iota(jnp.int32, (n, n_cols), 1)
                partner = at[0] + jnp.where(r < half, r, r - half + n_core)
                own_pair = (c == partner) & (s[:n] > 0.1 * masked_score)
                w = jnp.concatenate([w[:n] - jnp.where(own_pair, 2.0, 0.0), w[n:]], 0)
            w = w.astype(bf16)
            weights[t * part : (t + 1) * part, :] = w
            g = jnp.dot(w[:, :n_core], own[...], preferred_element_type=f32)
            g = g + jnp.dot(w[:, n_core:], other[...], preferred_element_type=f32)
            grads[t][...] = g.astype(bf16)

    out = (shaped((n_parts * part, n_cols), bf16),) + (shaped((part, width), bf16),) * n_parts
    at = jnp.reshape(start, (1,)).astype(jnp.int32)
    n_rows = n_parts * part
    cost = pl.CostEstimate(
        flops=2 * n_rows * n_cols * width, bytes_accessed=8 * n_rows * n_cols, transcendentals=0
    )
    return call(kernel, out, [at, scores, row_lse, col_lse] + list(cols), 1, cost=cost)


def col_products(weights, rows):
    part, width = rows[0].shape
    n_rows, n_cols = weights.shape
    n_core = n_cols // NC
    step = min(256, n_core)

    def kernel(w, *refs):
        row_refs, (own, other) = refs[: len(rows)], refs[len(rows) :]
        for j in range(n_cols // step):
            total = None
            for t, row in enumerate(row_refs):
                term = lax.dot_general(
                    w[t * part : (t + 1) * part, j * step : (j + 1) * step],
                    row[...],
                    (((0,), (0,)), ((), ())),
                    preferred_element_type=f32,
                )
                total = term if total is None else total + term
            place = j * step % n_core
            if j * step < n_core:
                own[place : place + step, :] = total
            else:
                other[place : place + step, :] = total.astype(bf16)

    out = (shaped((n_core, width), f32), shaped((n_core, width), bf16))
    cost = pl.CostEstimate(
        flops=2 * n_rows * n_cols * width, bytes_accessed=8 * n_rows * n_cols, transcendentals=0
    )
    return call(kernel, out, [weights] + list(rows), cost=cost)


def structure_parts(raw, own, got, coef):
    n_rows, width = raw.shape
    local, feats = n_rows // NR, width // NM

    def kernel(scale, raw_ref, own_ref, got_ref, out):
        for r in range(NR):
            rows = slice(r * local, (r + 1) * local)
            wide = raw_ref[rows].astype(f32)
            grads = scale[0] * (own_ref[rows] + got_ref[rows].astype(f32))
            squares = jnp.sum(wide * wide, 1, keepdims=True)
            inverse = 1.0 / jnp.sqrt(squares + epsilon)
            unit = wide * inverse
            dots = jnp.sum(unit * grads, 1, keepdims=True)
            done = (grads - unit * dots) * inverse
            for m in range(NM):
                start = (r * NM + m) * local
                out[start : start + local, :] = done[:, m * feats : (m + 1) * feats].astype(bf16)

    out = shaped((NZ * local, feats), bf16)
    return call(kernel, out, [jnp.reshape(coef, (1,)), raw, own, got], 1)


def from_chips_of_mp(wide, y_at, mp_at):
    def send(v, sources, d):
        pairs = [
            (dp_index(m + k, x, c) * NM + m, dp_index(m + k + d, x, c) * NM + m)
            for m in range(NM)
            for k in sources
            for x in range(NX)
            for c in range(NC)
        ]
        return lax.ppermute(v, ("dp", "mp"), pairs)

    away = (y_at - mp_at) % NY
    first = lambda v: jnp.where(away == 0, v, 0) + send(v, (0,), 2)
    second = lambda v: v + send(v, (0, 2), 1)
    return first, second


def to_owners(blocks, c_at, rep_at):
    own = block_at(blocks, c_at, 0, NC)
    other = block_at(blocks, 1 - c_at, 0, NC)

    def send(v, here, there):
        pairs = [
            (dp_index(y, x, k) * NR + here(k), dp_index(y, x, there(k)) * NR + k)
            for y in range(NY)
            for x in range(NX)
            for k in range(NC)
        ]
        return lax.ppermute(v, ("dp", "rep"), pairs)

    total = jnp.where(c_at == rep_at, own, 0.0)
    total = total + send(own, lambda k: 1 - k, lambda k: k)
    total = total + send(other, lambda k: 1 - k, lambda k: 1 - k)
    return total + send(other, lambda k: k, lambda k: 1 - k)


def body(emb_a, emb_b, keep, loss_scale, hidden_a, proj_a):
    dp_at = lax.axis_index("dp")
    mp_at = lax.axis_index("mp")
    rep_at = lax.axis_index("rep")
    y_at, x_at, c_at = dp_at // (NX * NC), dp_at // NC % NX, dp_at % NC
    local = emb_a.shape[0]
    piece = local // NM

    z_at = rep_at * NM + mp_at
    ring = ("rep", "mp")

    marked_b = jnp.where(keep[:, None] > 0, emb_b, jnp.array(8.0, bf16))
    own_block = jnp.concatenate([marked_b, proj_a], 0)
    gathered = lax.all_gather(own_block, ring)
    parts = [block_at(emb_a, mp_at, 0, NM)]
    for k in (1, 2, 3):
        parts.append(from_mp(block_at(emb_a, mp_at + NM - k, 0, NM), k))
    wide_a = turned(parts, NM - mp_at, 1).astype(f32)
    norms_a, units_a = normalize(wide_a)
    marker = jnp.where(jnp.arange(wide_a.shape[-1]) == 0, 2.0, 0.0).astype(bf16)[None, :]
    marked_a = jnp.where(block_at(keep, mp_at, 0, NM)[:, None] > 0, units_a, marker)
    chip_piece = jnp.concatenate(
        [block_at(marked_a, c_at, 0, NC), from_core(block_at(marked_a, 1 - c_at, 0, NC))], 0
    )
    line = line_gather(chip_piece)
    rows_u = [line] + [from_second(line, d) for d in OFFSETS[1:]]
    cols_own, raw_b, proj_ring = structure_units(tied(gathered, rows_u), local)
    cols_u = [cols_own, from_core(cols_own)]

    proj_1, proj_2 = from_chips_of_mp(proj_ring, y_at, mp_at)
    proj_rows = proj_1(tied(proj_ring, cols_u))
    scores, row_lse, col_info = masked_scores(rows_u, cols_u)
    row_lse, col_info = row_lse.reshape(-1), col_info.reshape(-1)
    proj_rows = proj_2(tied(proj_rows, row_lse))
    rows_of_chips = [[y * NX * NC + i for i in range(NX * NC)] for y in range(NY)]
    proj_rows = lax.all_gather(proj_rows, "dp", axis=0, tiled=True, axis_index_groups=rows_of_chips)
    for axis, d, col_step in ((1, 1, 1), (1, 2, 2), (0, 1, 4), (0, 2, 0)):
        row_other = (from_first if axis else from_second)(row_lse, d)
        col_other = from_z(col_info, col_step) if col_step else cols_swapped(from_core(col_info))
        row_lse = log_add(row_lse, rows_aligned(row_other, axis, d))
        col_info = log_add(col_info, col_other)
    count = jnp.exp(col_info[-1])
    coef = loss_scale[0] * logit_scale / (2.0 * count)

    half = piece // NC
    weights, *row_grads = weights_and_row_grads(
        scores, row_lse[None], col_info[None], cols_u, z_at * piece + c_at * half, half
    )
    line_a = line_sum(row_grads)
    col_own, col_other = col_products(weights, rows_u)
    col_got = from_core(col_other)
    low = tied(line_a.astype(bf16), col_own)
    grads_a = coef * piece_sum(line_a, low)
    got = from_core(grads_a[half:])
    first = c_at == 0
    grads_a = jnp.concatenate(
        [jnp.where(first, grads_a[:half], got), jnp.where(first, got, grads_a[:half])], 0
    )
    grad_a = unit_backward(grads_a, wide_a, norms_a).astype(bf16)

    pieces = [grad_a] + [from_mp(grad_a, -k) for k in (1, 2, 3)]
    mine = jnp.concatenate([block_at(p, mp_at, 1, NM) for p in pieces], 0)
    partial_b = structure_parts(raw_b, col_own, col_got, coef)
    grad_emb_b = lax.psum_scatter(partial_b, ring, scatter_dimension=0, tiled=True)
    hidden_t = hidden_prepared(hidden_a, y_at, x_at, c_at, mp_at)
    n_out = NX * NY * NC * NR * proj_a.shape[0]
    proj_part = jnp.dot(
        hidden_t.reshape(n_out, local), mine, preferred_element_type=f32
    ).reshape(NR, n_out // NR, -1)
    chip_part = proj_part[0] + from_core(proj_part[1].astype(bf16)).astype(f32)
    chip_part = chip_part.astype(bf16)
    n_line = chip_part.shape[0] // 4
    line_p = line_sum([chip_part[i * n_line : (i + 1) * n_line] for i in range(4)])

    rows_a = turned([pieces[-k % NM] for k in range(NM)], NM - mp_at, 0)
    grad_hidden = lax.dot_general(
        rows_a, proj_rows, (((1,), (1,)), ((), ())), preferred_element_type=f32
    ).astype(bf16)
    low = tied(line_p.astype(bf16), grad_hidden)
    owned = piece_sum(line_p, low)
    grad_proj = to_owners(owned, c_at, rep_at)
    return (grad_hidden, grad_proj, grad_emb_b)


def solution(mesh):
    return jax.shard_map(
        body,
        mesh=mesh,
        in_specs=(
            P(("dp", "rep"), "mp"),
            P(("dp", "rep"), "mp"),
            P(("dp", "rep")),
            P(),
            P(("dp", "rep"), None),
            P(("dp", "rep"), "mp"),
        ),
        out_specs=(P(("dp", "rep"), "mp"), P(("dp", "rep"), "mp"), P(("dp", "rep"), "mp")),
        check_vma=False,
    )
```

```python
import jax
import jax.numpy as jnp
from jax import lax
from jax.experimental import pallas as pl
from jax.experimental.pallas import tpu as pltpu
from jax.sharding import PartitionSpec as P

logit_scale = 100.0
masked_score = -1e30
epsilon = 1e-06
NX, NY, NC = 4, 4, 2
NM, NR = 4, 2
NZ = NM * NR
bf16 = jnp.bfloat16
f32 = jnp.float32


def dp_index(y, x, c):
    return ((y % NY) * NX + x % NX) * NC + c % NC


def dp_perm(to):
    return [
        (dp_index(y, x, c), dp_index(*to(y, x, c)))
        for y in range(NY)
        for x in range(NX)
        for c in range(NC)
    ]


def z_index(z):
    z = z % NZ
    return (z % NM) * NR + z // NM


def shift_perm(d, swapped):
    return dp_perm(
        lambda y, x, c: (y, x - d, c) if (c == 0) != swapped else (y - d, x, c)
    )


def from_first(v, d):
    return lax.ppermute(v, "dp", shift_perm(d, False))


def from_second(v, d):
    return lax.ppermute(v, "dp", shift_perm(d, True))


def from_x(v, d):
    return lax.ppermute(v, "dp", dp_perm(lambda y, x, c: (y, x - d, c)))


def from_core(v):
    return lax.ppermute(v, "dp", dp_perm(lambda y, x, c: (y, x, 1 - c)))


def from_z(v, d):
    return lax.ppermute(v, ("mp", "rep"), [(z_index(z), z_index(z - d)) for z in range(NZ)])


def from_mp(v, d):
    return lax.ppermute(v, "mp", [(m, (m - d) % NM) for m in range(NM)])


OFFSETS = (0, 1, 2, -1)


def tied(value, *others):
    return lax.optimization_barrier((value, others))[0]


def line_gather(piece):
    return jnp.concatenate([piece] + [from_first(piece, d) for d in OFFSETS[1:]], 0)


def line_received(blocks):
    return [from_second(blocks[i], -OFFSETS[i]) for i in (1, 2, 3)]


def line_added(own, got):
    size = own.shape[0] // 4

    def kernel(own_ref, got_1, got_2, got_3, first, *others):
        for i, out in enumerate((first,) + others):
            rows = slice(i * size, (i + 1) * size)
            total = own_ref[rows, :].astype(f32)
            for g in (got_1, got_2, got_3):
                total = total + g[rows, :].astype(f32)
            out[...] = total.astype(out.dtype)

    shape = (size, own.shape[1])
    return call(kernel, (shaped(shape, f32),) + (shaped(shape, bf16),) * 3, [own] + got)


def piece_received(parts):
    return [from_first(parts[i - 1], -OFFSETS[i]) for i in (1, 2, 3)]


def halves_added(own, got):
    half = own.shape[0] // NC

    def kernel(own_ref, got_1, got_2, got_3, *outs):
        for i, out in enumerate(outs):
            rows = slice(i * half, (i + 1) * half)
            total = own_ref[rows, :]
            for g in (got_1, got_2, got_3):
                total = total + g[rows, :].astype(f32)
            out[...] = total

    return call(kernel, (shaped((half, own.shape[1]), f32),) * NC, [own] + got)


def spectrum_finished(own, got, wide, coef, c_at):
    half = own.shape[0]

    def kernel(scale, at, own_ref, got_ref, wide_ref, out):
        first = at[0] == 0
        for i in range(NC):
            rows = slice(i * half, (i + 1) * half)
            a, b = (own_ref, got_ref) if i == 0 else (got_ref, own_ref)
            grads = scale[0] * jnp.where(first, a[...], b[...])
            values = wide_ref[rows, :]
            inverse = 1.0 / jnp.sqrt(jnp.sum(values * values, 1, keepdims=True) + epsilon)
            unit = values * inverse
            dots = jnp.sum(unit * grads, 1, keepdims=True)
            out[rows, :] = ((grads - unit * dots) * inverse).astype(bf16)

    at = jnp.reshape(c_at, (1,)).astype(jnp.int32)
    args = [jnp.reshape(coef, (1,)), at, own, got, wide]
    return call(kernel, shaped(wide.shape, bf16), args, 2)


def proj_products(hidden, pieces, mp_at):
    _, n_rows, _ = hidden.shape
    feats = pieces[0].shape[1] // NM
    step = 512

    def kernel(at, hidden_ref, *refs):
        ins, (own, other) = refs[:NM], refs[NM:]
        cols = pl.ds(pl.multiple_of(at[0] * feats, feats), feats)
        mine = jnp.concatenate([p[:, cols] for p in ins], 0)
        for i, out in enumerate((own, other)):
            for j in range(0, n_rows, step):
                g = jnp.dot(hidden_ref[i, j : j + step], mine, preferred_element_type=f32)
                out[j : j + step, :] = g.astype(out.dtype)

    out = (shaped((n_rows, feats), f32), shaped((n_rows, feats), bf16))
    at = jnp.reshape(mp_at, (1,)).astype(jnp.int32)
    return call(kernel, out, [at, hidden] + list(pieces), 1)


def quarters_added(own, got):
    size = own.shape[0] // 4

    def kernel(own_ref, got_ref, *outs):
        for i, out in enumerate(outs):
            rows = slice(i * size, (i + 1) * size)
            out[...] = (own_ref[rows, :] + got_ref[rows, :].astype(f32)).astype(bf16)

    return call(kernel, (shaped((size, own.shape[1]), bf16),) * 4, [own, got])


def hidden_gradient(pieces, proj, mp_at):
    rows, width = pieces[0].shape

    def kernel(at, proj_ref, *refs):
        ins, out = refs[:NM], refs[NM]
        wide = jnp.concatenate([p[...] for p in ins], 0)
        g = lax.dot_general(
            wide, proj_ref[...], (((1,), (1,)), ((), ())), preferred_element_type=f32
        ).astype(bf16)
        for k in range(NM):
            place = lax.rem(at[0] + NM - k, NM) * rows
            out[pl.ds(pl.multiple_of(place, rows), rows), :] = g[k * rows : (k + 1) * rows]

    out = shaped((NM * rows, proj.shape[0]), bf16)
    at = jnp.reshape(mp_at, (1,)).astype(jnp.int32)
    cost = pl.CostEstimate(
        flops=2 * NM * rows * width * proj.shape[0], bytes_accessed=2 * proj.size, transcendentals=0
    )
    return call(kernel, out, [at, proj] + list(pieces), 1, cost=cost)


def turned(blocks, shift, axis):
    n = len(blocks)
    size = blocks[0].shape[axis]
    doubled = jnp.concatenate(list(blocks) + list(blocks)[:-1], axis)
    return lax.dynamic_slice_in_dim(doubled, shift % n * size, n * size, axis)


def block_at(v, index, axis, n):
    size = v.shape[axis] // n
    return lax.dynamic_slice_in_dim(v, index % n * size, size, axis)


def rows_aligned(v, axis, d):
    return jnp.roll(v.reshape(4, 4, -1), d, axis).reshape(v.shape)


def cols_swapped(v):
    n = 128 * (v.shape[0] // 128 - 1) // 2
    return jnp.concatenate([v[n : 2 * n], v[:n], v[2 * n :]])


def log_add(a, b):
    return jnp.maximum(a, b) + jnp.log1p(jnp.exp(-jnp.abs(a - b)))


def normalize(wide):
    norms = jnp.sqrt(jnp.sum(wide * wide, axis=-1) + epsilon)
    return norms, (wide / norms[..., None]).astype(bf16)


def unit_backward(grads, wide, norms):
    unit = wide / norms[..., None]
    dots = jnp.sum(unit * grads, axis=-1)
    return (grads - unit * dots[..., None]) / norms[..., None]


def hidden_prepared(hidden, y_at, x_at, c_at, mp_at):
    rows, width = hidden.shape
    wide = width // (NX * NY * NC)
    half = wide // NR

    def kernel(at, hidden_ref, out_ref, turned_ref):
        piece = rows // NM
        core = at[2]
        for k in range(NM):
            source = lax.rem(at[3] + NM - k, NM)
            turned_ref[k * piece : (k + 1) * piece, :] = hidden_ref[
                pl.ds(pl.multiple_of(source * piece, piece), piece), :
            ]
        for i, dy in enumerate(OFFSETS):
            for j, dx in enumerate(OFFSETS):
                y = lax.rem(at[0] + NY + dy, NY)
                x = lax.rem(at[1] + NX + dx, NX)
                for c in range(NC):
                    column = ((y * NX + x) * NC + c) * wide
                    block = turned_ref[:, pl.ds(pl.multiple_of(column, wide), wide)]
                    block = block.astype(f32).T.astype(bf16)
                    for r in range(NR):
                        place = i * NX + j if r == 0 else j * NY + i
                        slot = lax.rem(core + r, NR)
                        out_ref[slot, place, c] = block[r * half : (r + 1) * half]

    return pl.pallas_call(
        kernel,
        out_shape=jax.ShapeDtypeStruct((NR, NX * NY, NC, half, rows), bf16),
        in_specs=[
            pl.BlockSpec(memory_space=pltpu.SMEM),
            pl.BlockSpec(memory_space=pltpu.VMEM),
        ],
        out_specs=pl.BlockSpec(memory_space=pltpu.VMEM),
        scratch_shapes=[pltpu.VMEM((rows, width), bf16)],
        compiler_params=pltpu.CompilerParams(vmem_limit_bytes=24 * 2**20),
    )(jnp.stack([y_at, x_at, c_at, mp_at]).astype(jnp.int32), hidden)


def call(kernel, out_shape, args, smem=0, far=(), far_out=(), scratch=(), vmem=8, cost=None):
    spaces = [pltpu.SMEM if i < smem else pltpu.HBM if i in far else pltpu.VMEM for i in range(len(args))]
    specs = [pl.BlockSpec(memory_space=space) for space in spaces]
    several = isinstance(out_shape, tuple)
    n_out = len(out_shape) if several else 1
    outs = [pl.BlockSpec(memory_space=pltpu.HBM if i in far_out else pltpu.VMEM) for i in range(n_out)]
    return pl.pallas_call(
        kernel,
        out_shape=out_shape,
        in_specs=specs,
        out_specs=tuple(outs) if several else outs[0],
        scratch_shapes=list(scratch),
        cost_estimate=cost,
        compiler_params=pltpu.CompilerParams(vmem_limit_bytes=vmem * 2**20),
    )(*args)


def copies(pairs, sems, first=0):
    started = [
        pltpu.make_async_copy(a, b, sems.at[first + i]) for i, (a, b) in enumerate(pairs)
    ]
    for c in started:
        c.start()
    return started


def shaped(shape, dtype):
    return jax.ShapeDtypeStruct(shape, dtype)


def structure_block(keep, emb, proj):
    local, feats = emb.shape
    extra = proj.shape[0]

    def kernel(keep_ref, emb_ref, proj_ref, out, held, sems):
        loads = copies(
            [(emb_ref, held.at[pl.ds(0, local)]), (proj_ref, held.at[pl.ds(local, extra)])], sems
        )
        kept = jnp.broadcast_to(keep_ref[...].astype(f32), (128, local)).T[:, :1] > 0.5
        loads[0].wait()
        held[:local, :] = jnp.where(kept, held[:local, :].astype(f32), 8.0).astype(bf16)
        loads[1].wait()
        store = copies([(held, out)], sems, 2)[0]
        store.wait()

    scratch = [pltpu.VMEM((local + extra, feats), bf16), pltpu.SemaphoreType.DMA((3,))]
    out = shaped((local + extra, feats), bf16)
    return call(kernel, out, [keep[None], emb, proj], far=(1, 2), far_out=(0,), scratch=scratch)


def structure_units(blocks, local):
    _, height, feats = blocks.shape
    extra = height - local

    def kernel(held, units, proj):
        for r in range(NR):
            rows = slice(r * local, (r + 1) * local)
            wide = [held[r * NM + m, :local].astype(f32) for m in range(NM)]
            squares = sum(jnp.sum(w * w, 1, keepdims=True) for w in wide)
            inverse = 1.0 / jnp.sqrt(squares + epsilon)
            dropped = wide[0][:, :1] > 4.0
            lane = lax.broadcasted_iota(jnp.int32, (local, feats), 1)
            for m in range(NM):
                cols = slice(m * feats, (m + 1) * feats)
                marker = jnp.where(lane == 0, 2.0, 0.0) if m == 0 else jnp.zeros_like(wide[m])
                units[rows, cols] = jnp.where(dropped, marker, wide[m] * inverse).astype(bf16)
                proj[r * extra : (r + 1) * extra, cols] = held[r * NM + m, local:]

    out = (shaped((NR * local, NM * feats), bf16), shaped((NR * extra, NM * feats), bf16))
    return call(kernel, out, [blocks], vmem=10)


def block_copied(blocks, index):
    def kernel(at, blocks_ref, out, sems):
        copies([(blocks_ref.at[at[0]], out)], sems)[0].wait()

    at = jnp.reshape(index, (1,)).astype(jnp.int32)
    scratch = [pltpu.SemaphoreType.DMA((1,))]
    return call(kernel, shaped(blocks.shape[1:], bf16), [at, blocks], 1, (1,), (0,), scratch, 1)


def scores_of(row, cols, kept_cols):
    nt = (((1,), (1,)), ((), ()))
    kept_rows = row[:, :1].astype(f32) < 1.5
    s = [lax.dot_general(row, c[...], nt, preferred_element_type=f32) for c in cols]
    s = logit_scale * jnp.concatenate(s, 1)
    return jnp.where(kept_rows & kept_cols, s, masked_score), kept_rows


def score_sums(rows, cols):
    part, width = rows[0].shape
    n_rows, n_cols = len(rows) * part, sum(c.shape[0] for c in cols)

    def kernel(*refs):
        col_refs, (row_out, col_out, kept_out) = refs[len(rows) :][: len(cols)], refs[-4:-1]
        row_refs, scores = refs[: len(rows)], refs[-1]
        first = (lax.broadcasted_iota(jnp.int32, (16, width), 1) == 0).astype(f32).astype(bf16)
        nt = (((1,), (1,)), ((), ()))
        marks = [lax.dot_general(first, c[...], nt, preferred_element_type=f32) for c in col_refs]
        kept_cols = jnp.concatenate(marks, 1)[:1] < 1.5
        kept_out[...] = kept_cols.astype(f32)
        col_top = None
        count = jnp.zeros((1, 1), f32)
        for t in range(len(rows)):
            s, kept_rows = scores_of(row_refs[t][...], col_refs, kept_cols)
            count = count + jnp.sum(kept_rows.astype(f32), 0, keepdims=True)
            scores[t] = s
            top = jnp.max(s, 1, keepdims=True)
            lse = top + jnp.log(jnp.sum(jnp.exp(s - top), 1, keepdims=True))
            row_out[:, t * part : (t + 1) * part] = jnp.broadcast_to(lse, (part, 128)).T[:1]
            here = jnp.max(s, 0, keepdims=True)
            col_top = here if col_top is None else jnp.maximum(col_top, here)
        total = jnp.zeros_like(col_top)
        for t in range(len(rows)):
            total = total + jnp.sum(jnp.exp(scores[t] - col_top), 0, keepdims=True)
        col_out[:, :n_cols] = col_top + jnp.log(total)
        col_out[:, n_cols:] = jnp.broadcast_to(jnp.log(count), (1, 128))

    out = (shaped((1, n_rows), f32), shaped((1, n_cols + 128), f32), shaped((1, n_cols), f32))
    cost = pl.CostEstimate(
        flops=2 * n_rows * n_cols * width, bytes_accessed=8 * n_rows * n_cols, transcendentals=0
    )
    scratch = [
        pltpu.VMEM((len(rows), part, n_cols), f32),
    ]
    args = list(rows) + list(cols)
    return call(kernel, out, args, scratch=scratch, vmem=16, cost=cost)


def weights_and_row_grads(row_units, kept, row_lse, col_lse, cols, start, half):
    part, width = row_units.shape
    n_cols = kept.shape[1]
    n_core = n_cols // NC
    n_chunks = 2
    chunk = part // n_chunks

    def kernel(at, units_ref, kept_ref, row_ref, col_ref, own, other, weights, grads, *refs):
        held, w_held, g_held, sems = refs
        place = [pl.ds(i * chunk, chunk) for i in range(n_chunks)]
        loads = copies([(units_ref.at[p], held.at[p]) for p in place], sems)
        stores = []
        col = jnp.maximum(col_ref[:, :n_cols], 0.1 * masked_score)
        row = jnp.maximum(row_ref[...], 0.1 * masked_score)
        row = jnp.broadcast_to(row, (128, part)).T[:, :1]
        kept_cols = kept_ref[...] > 0.5
        for i, p in enumerate(place):
            loads[i].wait()
            rows = slice(i * chunk, (i + 1) * chunk)
            s, _ = scores_of(held[rows, :], (own, other), kept_cols)
            w = jnp.exp(s - row[rows]) + jnp.exp(s - col)
            if i == 0 and half:
                n = NC * half
                r = lax.broadcasted_iota(jnp.int32, (n, n_cols), 0)
                c = lax.broadcasted_iota(jnp.int32, (n, n_cols), 1)
                partner = at[0] + jnp.where(r < half, r, r - half + n_core)
                own_pair = (c == partner) & (s[:n] > 0.1 * masked_score)
                w = jnp.concatenate([w[:n] - jnp.where(own_pair, 2.0, 0.0), w[n:]], 0)
            w = w.astype(bf16)
            w_held[rows, :] = w
            g = jnp.dot(w[:, :n_core], own[...], preferred_element_type=f32)
            g = g + jnp.dot(w[:, n_core:], other[...], preferred_element_type=f32)
            g_held[rows, :] = g.astype(bf16)
            stores += copies([(g_held.at[p], grads.at[p])], sems, n_chunks + i)
            stores += copies([(w_held.at[p], weights.at[p])], sems, 2 * n_chunks + i)
        for store in stores:
            store.wait()

    out = (shaped((part, n_cols), bf16), shaped((part, width), bf16))
    at = jnp.reshape(start, (1,)).astype(jnp.int32)
    cost = pl.CostEstimate(
        flops=4 * part * n_cols * width, bytes_accessed=8 * part * n_cols, transcendentals=0
    )
    scratch = [
        pltpu.VMEM((part, width), bf16),
        pltpu.VMEM((part, n_cols), bf16),
        pltpu.VMEM((part, width), bf16),
        pltpu.SemaphoreType.DMA((3 * n_chunks,)),
    ]
    args = [at, row_units, kept, row_lse, col_lse] + list(cols)
    return call(kernel, out, args, 1, (1,), (0, 1), scratch, 10, cost)


def col_products(weights, rows):
    part, width = rows[0].shape
    n_cols = weights[0].shape[1]
    n_parts = len(rows)
    n_core = n_cols // NC
    step = min(256, n_core)

    def kernel(*refs):
        own, other, w, row_refs, sems = refs[2 * n_parts :]
        loads = copies([(refs[t], w.at[t]) for t in range(n_parts)], sems)
        loads += copies([(refs[n_parts + t], row_refs.at[t]) for t in range(n_parts)], sems, n_parts)
        for load in loads:
            load.wait()
        for j in range(n_cols // step):
            total = None
            for t in range(n_parts):
                term = lax.dot_general(
                    w[t, :, j * step : (j + 1) * step],
                    row_refs[t],
                    (((0,), (0,)), ((), ())),
                    preferred_element_type=f32,
                )
                total = term if total is None else total + term
            place = j * step % n_core
            if j * step < n_core:
                own[place : place + step, :] = total
            else:
                other[place : place + step, :] = total.astype(bf16)

    out = (shaped((n_core, width), f32), shaped((n_core, width), bf16))
    cost = pl.CostEstimate(
        flops=2 * n_parts * part * n_cols * width, bytes_accessed=8 * part * n_cols, transcendentals=0
    )
    scratch = [
        pltpu.VMEM((n_parts, part, n_cols), bf16),
        pltpu.VMEM((n_parts, part, width), bf16),
        pltpu.SemaphoreType.DMA((2 * n_parts,)),
    ]
    args = list(weights) + list(rows)
    return call(kernel, out, args, far=range(2 * n_parts), scratch=scratch, vmem=20, cost=cost)


def structure_parts(blocks, own, got, coef, local):
    feats = blocks.shape[2]

    def kernel(scale, blocks_ref, own_ref, got_ref, out, held, sems):
        loads = copies(
            [(blocks_ref.at[z, pl.ds(0, local)], held.at[z]) for z in range(NZ)], sems
        )
        for r in range(NR):
            for m in range(NM):
                loads[r * NM + m].wait()
            rows = slice(r * local, (r + 1) * local)
            wide = [held[r * NM + m].astype(f32) for m in range(NM)]
            grads = scale[0] * (own_ref[rows] + got_ref[rows].astype(f32))
            grads = [grads[:, m * feats : (m + 1) * feats] for m in range(NM)]
            squares = sum(jnp.sum(w * w, 1, keepdims=True) for w in wide)
            inverse = 1.0 / jnp.sqrt(squares + epsilon)
            dots = sum(jnp.sum(w * g, 1, keepdims=True) for w, g in zip(wide, grads))
            dots = dots * inverse * inverse
            for m in range(NM):
                start = (r * NM + m) * local
                done = (grads[m] - wide[m] * dots) * inverse
                out[start : start + local, :] = done.astype(bf16)

    out = shaped((NZ * local, feats), bf16)
    scratch = [pltpu.VMEM((NZ, local, feats), bf16), pltpu.SemaphoreType.DMA((NZ,))]
    args = [jnp.reshape(coef, (1,)), blocks, own, got]
    return call(kernel, out, args, 1, (1,), (), scratch, 16)


def to_owners(blocks, c_at, rep_at, meanwhile):
    half = blocks.shape[0] // NC
    pairs = [
        (dp_index(y, x, k) * NR + 1 - k, dp_index(y, x, k) * NR + k)
        for y in range(NY)
        for x in range(NX)
        for k in range(NC)
    ]
    got = tied(lax.ppermute(blocks.astype(bf16), ("dp", "rep"), pairs), meanwhile)
    total = blocks + got.astype(f32)
    first = c_at == 0
    own = jnp.where(first, total[:half], total[half:])
    got = from_core(jnp.where(first, total[half:], total[:half]))
    return jnp.where(c_at == rep_at, own, got)


def body(emb_a, emb_b, keep, loss_scale, hidden_a, proj_a):
    dp_at = lax.axis_index("dp")
    mp_at = lax.axis_index("mp")
    rep_at = lax.axis_index("rep")
    y_at, x_at, c_at = dp_at // (NX * NC), dp_at // NC % NX, dp_at % NC
    local = emb_a.shape[0]
    piece = local // NM

    z_at = rep_at * NM + mp_at
    ring = ("rep", "mp")

    own_block = structure_block(keep, emb_b, proj_a)
    gathered = lax.all_gather(own_block, ring)
    emb_a = tied(emb_a, own_block)
    parts = [block_at(emb_a, mp_at, 0, NM)]
    for k in (1, 2, 3):
        parts.append(from_mp(block_at(emb_a, mp_at + NM - k, 0, NM), k))
    wide_a = turned(parts, NM - mp_at, 1).astype(f32)
    _, units_a = normalize(wide_a)
    marker = jnp.where(jnp.arange(wide_a.shape[-1]) == 0, 2.0, 0.0).astype(bf16)[None, :]
    marked_a = jnp.where(block_at(keep, mp_at, 0, NM)[:, None] > 0, units_a, marker)
    chip_piece = jnp.concatenate(
        [block_at(marked_a, c_at, 0, NC), from_core(block_at(marked_a, 1 - c_at, 0, NC))], 0
    )
    line = line_gather(chip_piece)
    rows_u = [line] + [from_second(line, d) for d in OFFSETS[1:]]
    cols_own, proj_ring = structure_units(tied(gathered, rows_u), local)
    columns = [[y * NX * NC + i for y in range(NY)] for i in range(NX * NC)]
    rows_of_chips = [[y * NX * NC + i for i in range(NX * NC)] for y in range(NY)]
    proj_column = lax.all_gather(proj_ring, "dp", axis_index_groups=columns)
    cols_u = [cols_own, from_core(cols_own)]
    row_lse, col_info, kept_cols = score_sums(rows_u, cols_u)
    row_lse, col_info = row_lse.reshape(-1), col_info.reshape(-1)
    for axis, d, col_step in ((1, 1, 1), (1, 2, 2), (0, 1, 4), (0, 2, 0)):
        row_other = (from_first if axis else from_second)(row_lse, d)
        col_other = from_z(col_info, col_step) if col_step else cols_swapped(from_core(col_info))
        row_lse = log_add(row_lse, rows_aligned(row_other, axis, d))
        col_info = log_add(col_info, col_other)
    count = jnp.exp(col_info[-1])
    coef = loss_scale[0] * logit_scale / (2.0 * count)

    half = piece // NC
    start = z_at * piece + c_at * half
    weights, row_grads = [None] * 4, [None] * 4
    size = rows_u[0].shape[0]
    for t in (2, 1, 3, 0):
        weights[t], row_grads[t] = weights_and_row_grads(
            rows_u[t],
            kept_cols,
            row_lse[None, t * size : (t + 1) * size],
            col_info[None],
            cols_u,
            start,
            half if t == 0 else 0,
        )
    got = line_received(row_grads)
    col_own, col_other = col_products(weights, rows_u)
    got = tied(got, col_own)
    first_a, *parts_a = line_added(row_grads[0], got)
    proj_column = tied(proj_column, first_a)
    proj_rows = block_copied(proj_column, mp_at)
    proj_rows = lax.all_gather(proj_rows, "dp", axis=0, tiled=True, axis_index_groups=rows_of_chips)
    col_got = from_core(tied(col_other, first_a))
    parts_a = tied(parts_a, col_own)
    got = piece_received(parts_a)
    half_own, half_other = halves_added(first_a, got)
    grad_a = spectrum_finished(half_own, from_core(half_other), wide_a, coef, c_at)

    pieces = [grad_a] + [from_mp(grad_a, -k) for k in (1, 2, 3)]
    partial_b = structure_parts(gathered, tied(col_own, grad_a), col_got, coef, local)
    grad_emb_b = lax.psum_scatter(partial_b, ring, scatter_dimension=0, tiled=True)
    pieces = tied(pieces, partial_b)
    hidden_t = hidden_prepared(hidden_a, y_at, x_at, c_at, mp_at)
    proj_own, proj_other = proj_products(hidden_t.reshape(NR, -1, local), pieces, mp_at)
    chip_parts = quarters_added(proj_own, from_core(proj_other))
    got = line_received(chip_parts)
    grad_hidden = hidden_gradient(pieces, tied(proj_rows, chip_parts), mp_at)
    first_p, *parts_p = line_added(chip_parts[0], got)
    owned = sum([g.astype(f32) for g in piece_received(parts_p)], first_p)
    grad_proj = to_owners(owned, c_at, rep_at, (grad_hidden, grad_emb_b))
    return (grad_hidden, grad_proj, grad_emb_b)


def solution(mesh):
    return jax.shard_map(
        body,
        mesh=mesh,
        in_specs=(
            P(("dp", "rep"), "mp"),
            P(("dp", "rep"), "mp"),
            P(("dp", "rep")),
            P(),
            P(("dp", "rep"), None),
            P(("dp", "rep"), "mp"),
        ),
        out_specs=(P(("dp", "rep"), "mp"), P(("dp", "rep"), "mp"), P(("dp", "rep"), "mp")),
        check_vma=False,
    )
```

```python
import jax
import jax.numpy as jnp
from jax import lax
from jax.experimental import pallas as pl
from jax.experimental.pallas import tpu as pltpu
from jax.sharding import PartitionSpec as P

logit_scale = 100.0
masked_score = -1e30
epsilon = 1e-06
NX, NY, NC = 4, 4, 2
NM, NR = 4, 2
NZ = NM * NR
bf16 = jnp.bfloat16
f32 = jnp.float32


def dp_index(y, x, c):
    return ((y % NY) * NX + x % NX) * NC + c % NC


def dp_perm(to):
    return [
        (dp_index(y, x, c), dp_index(*to(y, x, c)))
        for y in range(NY)
        for x in range(NX)
        for c in range(NC)
    ]


def z_index(z):
    z = z % NZ
    return (z % NM) * NR + z // NM


def shift_perm(d, swapped):
    return dp_perm(
        lambda y, x, c: (y, x - d, c) if (c == 0) != swapped else (y - d, x, c)
    )


def from_first(v, d):
    return lax.ppermute(v, "dp", shift_perm(d, False))


def from_second(v, d):
    return lax.ppermute(v, "dp", shift_perm(d, True))


def from_core(v):
    return lax.ppermute(v, "dp", dp_perm(lambda y, x, c: (y, x, 1 - c)))


def from_z(v, d):
    return lax.ppermute(v, ("mp", "rep"), [(z_index(z), z_index(z - d)) for z in range(NZ)])


def from_mp(v, d):
    return lax.ppermute(v, "mp", [(m, (m - d) % NM) for m in range(NM)])


OFFSETS = (0, 1, 2, -1)


def tied(value, *others):
    return lax.optimization_barrier((value, others))[0]


def line_gather(piece):
    return jnp.concatenate([piece] + [from_first(piece, d) for d in OFFSETS[1:]], 0)


def line_received(blocks):
    return [from_second(blocks[i], -OFFSETS[i]) for i in (1, 2, 3)]


def line_added(own, got):
    size = own.shape[0] // 4

    def kernel(own_ref, got_1, got_2, got_3, first, *others):
        for i, out in enumerate((first,) + others):
            rows = slice(i * size, (i + 1) * size)
            total = own_ref[rows, :].astype(f32)
            for g in (got_1, got_2, got_3):
                total = total + g[rows, :].astype(f32)
            out[...] = total.astype(out.dtype)

    shape = (size, own.shape[1])
    return call(kernel, (shaped(shape, f32),) + (shaped(shape, bf16),) * 3, [own] + got)


def piece_received(parts):
    return [from_first(parts[i - 1], -OFFSETS[i]) for i in (1, 2, 3)]


def halves_added(own, got):
    half = own.shape[0] // NC

    def kernel(own_ref, got_1, got_2, got_3, *outs):
        for i, out in enumerate(outs):
            rows = slice(i * half, (i + 1) * half)
            total = own_ref[rows, :]
            for g in (got_1, got_2, got_3):
                total = total + g[rows, :].astype(f32)
            out[...] = total

    return call(kernel, (shaped((half, own.shape[1]), f32),) * NC, [own] + got)


def spectrum_finished(own, got, wide, coef, c_at):
    half = own.shape[0]

    def kernel(scale, at, own_ref, got_ref, wide_ref, out):
        first = at[0] == 0
        for i in range(NC):
            rows = slice(i * half, (i + 1) * half)
            a, b = (own_ref, got_ref) if i == 0 else (got_ref, own_ref)
            grads = scale[0] * jnp.where(first, a[...], b[...])
            values = wide_ref[rows, :]
            inverse = 1.0 / jnp.sqrt(jnp.sum(values * values, 1, keepdims=True) + epsilon)
            unit = values * inverse
            dots = jnp.sum(unit * grads, 1, keepdims=True)
            out[rows, :] = ((grads - unit * dots) * inverse).astype(bf16)

    at = jnp.reshape(c_at, (1,)).astype(jnp.int32)
    args = [jnp.reshape(coef, (1,)), at, own, got, wide]
    return call(kernel, shaped(wide.shape, bf16), args, 2)


def proj_products(hidden, pieces, mp_at):
    _, n_rows, _ = hidden.shape
    feats = pieces[0].shape[1] // NM
    step = 512

    def kernel(at, hidden_ref, *refs):
        ins, (own, other) = refs[:NM], refs[NM:]
        cols = pl.ds(pl.multiple_of(at[0] * feats, feats), feats)
        mine = jnp.concatenate([p[:, cols] for p in ins], 0)
        for i, out in enumerate((own, other)):
            for j in range(0, n_rows, step):
                g = jnp.dot(hidden_ref[i, j : j + step], mine, preferred_element_type=f32)
                out[j : j + step, :] = g.astype(out.dtype)

    out = (shaped((n_rows, feats), f32), shaped((n_rows, feats), bf16))
    at = jnp.reshape(mp_at, (1,)).astype(jnp.int32)
    return call(kernel, out, [at, hidden] + list(pieces), 1)


def quarters_added(own, got):
    size = own.shape[0] // 4

    def kernel(own_ref, got_ref, *outs):
        for i, out in enumerate(outs):
            rows = slice(i * size, (i + 1) * size)
            out[...] = (own_ref[rows, :] + got_ref[rows, :].astype(f32)).astype(bf16)

    return call(kernel, (shaped((size, own.shape[1]), bf16),) * 4, [own, got])


def hidden_gradient(pieces, proj, mp_at):
    rows, width = pieces[0].shape

    def kernel(at, proj_ref, *refs):
        ins, out = refs[:NM], refs[NM]
        wide = jnp.concatenate([p[...] for p in ins], 0)
        g = lax.dot_general(
            wide, proj_ref[...], (((1,), (1,)), ((), ())), preferred_element_type=f32
        ).astype(bf16)
        for k in range(NM):
            place = lax.rem(at[0] + NM - k, NM) * rows
            out[pl.ds(pl.multiple_of(place, rows), rows), :] = g[k * rows : (k + 1) * rows]

    out = shaped((NM * rows, proj.shape[0]), bf16)
    at = jnp.reshape(mp_at, (1,)).astype(jnp.int32)
    cost = pl.CostEstimate(
        flops=2 * NM * rows * width * proj.shape[0], bytes_accessed=2 * proj.size, transcendentals=0
    )
    return call(kernel, out, [at, proj] + list(pieces), 1, cost=cost)


def turned(blocks, shift, axis):
    n = len(blocks)
    size = blocks[0].shape[axis]
    doubled = jnp.concatenate(list(blocks) + list(blocks)[:-1], axis)
    return lax.dynamic_slice_in_dim(doubled, shift % n * size, n * size, axis)


def block_at(v, index, axis, n):
    size = v.shape[axis] // n
    return lax.dynamic_slice_in_dim(v, index % n * size, size, axis)


def rows_aligned(v, axis, d):
    return jnp.roll(v.reshape(4, 4, -1), d, axis).reshape(v.shape)


def cols_swapped(v):
    n = 128 * (v.shape[0] // 128 - 1) // 2
    return jnp.concatenate([v[n : 2 * n], v[:n], v[2 * n :]])


def log_add(a, b):
    return jnp.maximum(a, b) + jnp.log1p(jnp.exp(-jnp.abs(a - b)))


def normalize(wide):
    norms = jnp.sqrt(jnp.sum(wide * wide, axis=-1) + epsilon)
    return norms, (wide / norms[..., None]).astype(bf16)


def hidden_prepared(hidden, y_at, x_at, c_at, mp_at):
    rows, width = hidden.shape
    wide = width // (NX * NY * NC)
    half = wide // NR

    def kernel(at, hidden_ref, out_ref, turned_ref):
        piece = rows // NM
        core = at[2]
        for k in range(NM):
            source = lax.rem(at[3] + NM - k, NM)
            turned_ref[k * piece : (k + 1) * piece, :] = hidden_ref[
                pl.ds(pl.multiple_of(source * piece, piece), piece), :
            ]
        for i, dy in enumerate(OFFSETS):
            for j, dx in enumerate(OFFSETS):
                y = lax.rem(at[0] + NY + dy, NY)
                x = lax.rem(at[1] + NX + dx, NX)
                for c in range(NC):
                    column = ((y * NX + x) * NC + c) * wide
                    block = turned_ref[:, pl.ds(pl.multiple_of(column, wide), wide)]
                    block = block.astype(f32).T.astype(bf16)
                    for r in range(NR):
                        place = i * NX + j if r == 0 else j * NY + i
                        slot = lax.rem(core + r, NR)
                        out_ref[slot, place, c] = block[r * half : (r + 1) * half]

    return pl.pallas_call(
        kernel,
        out_shape=jax.ShapeDtypeStruct((NR, NX * NY, NC, half, rows), bf16),
        in_specs=[
            pl.BlockSpec(memory_space=pltpu.SMEM),
            pl.BlockSpec(memory_space=pltpu.VMEM),
        ],
        out_specs=pl.BlockSpec(memory_space=pltpu.VMEM),
        scratch_shapes=[pltpu.VMEM((rows, width), bf16)],
        compiler_params=pltpu.CompilerParams(vmem_limit_bytes=24 * 2**20),
    )(jnp.stack([y_at, x_at, c_at, mp_at]).astype(jnp.int32), hidden)


def call(kernel, out_shape, args, smem=0, far=(), far_out=(), scratch=(), vmem=8, cost=None):
    spaces = [pltpu.SMEM if i < smem else pltpu.HBM if i in far else pltpu.VMEM for i in range(len(args))]
    specs = [pl.BlockSpec(memory_space=space) for space in spaces]
    several = isinstance(out_shape, tuple)
    n_out = len(out_shape) if several else 1
    outs = [pl.BlockSpec(memory_space=pltpu.HBM if i in far_out else pltpu.VMEM) for i in range(n_out)]
    return pl.pallas_call(
        kernel,
        out_shape=out_shape,
        in_specs=specs,
        out_specs=tuple(outs) if several else outs[0],
        scratch_shapes=list(scratch),
        cost_estimate=cost,
        compiler_params=pltpu.CompilerParams(vmem_limit_bytes=vmem * 2**20),
    )(*args)


def copies(pairs, sems, first=0):
    started = [
        pltpu.make_async_copy(a, b, sems.at[first + i]) for i, (a, b) in enumerate(pairs)
    ]
    for c in started:
        c.start()
    return started


def shaped(shape, dtype):
    return jax.ShapeDtypeStruct(shape, dtype)


def structure_block(keep, emb, proj):
    local, feats = emb.shape
    extra = proj.shape[0]

    def kernel(keep_ref, emb_ref, proj_ref, out, held, sems):
        loads = copies(
            [(emb_ref, held.at[pl.ds(0, local)]), (proj_ref, held.at[pl.ds(local, extra)])], sems
        )
        kept = jnp.broadcast_to(keep_ref[...].astype(f32), (128, local)).T[:, :1] > 0.5
        loads[0].wait()
        held[:local, :] = jnp.where(kept, held[:local, :].astype(f32), 8.0).astype(bf16)
        loads[1].wait()
        store = copies([(held, out)], sems, 2)[0]
        store.wait()

    scratch = [pltpu.VMEM((local + extra, feats), bf16), pltpu.SemaphoreType.DMA((3,))]
    out = shaped((local + extra, feats), bf16)
    return call(kernel, out, [keep[None], emb, proj], far=(1, 2), far_out=(0,), scratch=scratch)


def structure_units(blocks, local):
    _, height, feats = blocks.shape
    extra = height - local

    def kernel(held, units, proj):
        for r in range(NR):
            rows = slice(r * local, (r + 1) * local)
            wide = [held[r * NM + m, :local].astype(f32) for m in range(NM)]
            squares = sum(jnp.sum(w * w, 1, keepdims=True) for w in wide)
            inverse = 1.0 / jnp.sqrt(squares + epsilon)
            dropped = wide[0][:, :1] > 4.0
            lane = lax.broadcasted_iota(jnp.int32, (local, feats), 1)
            for m in range(NM):
                cols = slice(m * feats, (m + 1) * feats)
                marker = jnp.where(lane == 0, 2.0, 0.0) if m == 0 else jnp.zeros_like(wide[m])
                units[rows, cols] = jnp.where(dropped, marker, wide[m] * inverse).astype(bf16)
                proj[r * extra : (r + 1) * extra, cols] = held[r * NM + m, local:]

    out = (shaped((NR * local, NM * feats), bf16), shaped((NR * extra, NM * feats), bf16))
    return call(kernel, out, [blocks], vmem=10)


def block_copied(blocks, index):
    def kernel(at, blocks_ref, out, sems):
        copies([(blocks_ref.at[at[0]], out)], sems)[0].wait()

    at = jnp.reshape(index, (1,)).astype(jnp.int32)
    scratch = [pltpu.SemaphoreType.DMA((1,))]
    return call(kernel, shaped(blocks.shape[1:], bf16), [at, blocks], 1, (1,), (0,), scratch, 1)


def scores_of(row, cols, kept_cols):
    nt = (((1,), (1,)), ((), ()))
    kept_rows = row[:, :1].astype(f32) < 1.5
    s = [lax.dot_general(row, c[...], nt, preferred_element_type=f32) for c in cols]
    s = logit_scale * jnp.concatenate(s, 1)
    return jnp.where(kept_rows & kept_cols, s, masked_score), kept_rows


def score_sums(rows, cols):
    part, width = rows[0].shape
    n_rows, n_cols = len(rows) * part, sum(c.shape[0] for c in cols)

    def kernel(*refs):
        col_refs, (row_out, col_out, kept_out) = refs[len(rows) :][: len(cols)], refs[-4:-1]
        row_refs, scores = refs[: len(rows)], refs[-1]
        first = (lax.broadcasted_iota(jnp.int32, (16, width), 1) == 0).astype(f32).astype(bf16)
        nt = (((1,), (1,)), ((), ()))
        marks = [lax.dot_general(first, c[...], nt, preferred_element_type=f32) for c in col_refs]
        kept_cols = jnp.concatenate(marks, 1)[:1] < 1.5
        kept_out[...] = kept_cols.astype(f32)
        col_top = None
        count = jnp.zeros((1, 1), f32)
        for t in range(len(rows)):
            s, kept_rows = scores_of(row_refs[t][...], col_refs, kept_cols)
            count = count + jnp.sum(kept_rows.astype(f32), 0, keepdims=True)
            scores[t] = s
            top = jnp.max(s, 1, keepdims=True)
            lse = top + jnp.log(jnp.sum(jnp.exp(s - top), 1, keepdims=True))
            row_out[:, t * part : (t + 1) * part] = jnp.broadcast_to(lse, (part, 128)).T[:1]
            here = jnp.max(s, 0, keepdims=True)
            col_top = here if col_top is None else jnp.maximum(col_top, here)
        total = jnp.zeros_like(col_top)
        for t in range(len(rows)):
            total = total + jnp.sum(jnp.exp(scores[t] - col_top), 0, keepdims=True)
        col_out[:, :n_cols] = col_top + jnp.log(total)
        col_out[:, n_cols:] = jnp.broadcast_to(jnp.log(count), (1, 128))

    out = (shaped((1, n_rows), f32), shaped((1, n_cols + 128), f32), shaped((1, n_cols), f32))
    cost = pl.CostEstimate(
        flops=2 * n_rows * n_cols * width, bytes_accessed=8 * n_rows * n_cols, transcendentals=0
    )
    scratch = [
        pltpu.VMEM((len(rows), part, n_cols), f32),
    ]
    args = list(rows) + list(cols)
    return call(kernel, out, args, scratch=scratch, vmem=16, cost=cost)


def weights_and_row_grads(row_units, kept, row_lse, col_lse, cols, start, half):
    part, width = row_units.shape
    n_cols = kept.shape[1]
    n_core = n_cols // NC
    n_chunks = 2
    chunk = part // n_chunks

    def kernel(at, units_ref, kept_ref, row_ref, col_ref, own, other, weights, grads):
        col = jnp.maximum(col_ref[:, :n_cols], 0.1 * masked_score)
        row = jnp.maximum(row_ref[...], 0.1 * masked_score)
        row = jnp.broadcast_to(row, (128, part)).T[:, :1]
        kept_cols = kept_ref[...] > 0.5
        for i in range(n_chunks):
            rows = slice(i * chunk, (i + 1) * chunk)
            s, _ = scores_of(units_ref[rows, :], (own, other), kept_cols)
            w = jnp.exp(s - row[rows]) + jnp.exp(s - col)
            if i == 0 and half:
                n = NC * half
                r = lax.broadcasted_iota(jnp.int32, (n, n_cols), 0)
                c = lax.broadcasted_iota(jnp.int32, (n, n_cols), 1)
                partner = at[0] + jnp.where(r < half, r, r - half + n_core)
                own_pair = (c == partner) & (s[:n] > 0.1 * masked_score)
                w = jnp.concatenate([w[:n] - jnp.where(own_pair, 2.0, 0.0), w[n:]], 0)
            w = w.astype(bf16)
            weights[rows, :] = w
            g = jnp.dot(w[:, :n_core], own[...], preferred_element_type=f32)
            g = g + jnp.dot(w[:, n_core:], other[...], preferred_element_type=f32)
            grads[rows, :] = g.astype(bf16)

    out = (shaped((part, n_cols), bf16), shaped((part, width), bf16))
    at = jnp.reshape(start, (1,)).astype(jnp.int32)
    cost = pl.CostEstimate(
        flops=4 * part * n_cols * width, bytes_accessed=8 * part * n_cols, transcendentals=0
    )
    args = [at, row_units, kept, row_lse, col_lse] + list(cols)
    return call(kernel, out, args, 1, vmem=10, cost=cost)


def col_products(weights, rows):
    part, width = rows[0].shape
    n_cols = weights[0].shape[1]
    n_parts = len(rows)
    n_core = n_cols // NC
    step = min(256, n_core)

    def kernel(*refs):
        own, other, w, row_refs, sems = refs[2 * n_parts :]
        loads = copies([(refs[t], w.at[t]) for t in range(n_parts)], sems)
        loads += copies([(refs[n_parts + t], row_refs.at[t]) for t in range(n_parts)], sems, n_parts)
        for load in loads:
            load.wait()
        for j in range(n_cols // step):
            total = None
            for t in range(n_parts):
                term = lax.dot_general(
                    w[t, :, j * step : (j + 1) * step],
                    row_refs[t],
                    (((0,), (0,)), ((), ())),
                    preferred_element_type=f32,
                )
                total = term if total is None else total + term
            place = j * step % n_core
            if j * step < n_core:
                own[place : place + step, :] = total
            else:
                other[place : place + step, :] = total.astype(bf16)

    out = (shaped((n_core, width), f32), shaped((n_core, width), bf16))
    cost = pl.CostEstimate(
        flops=2 * n_parts * part * n_cols * width, bytes_accessed=8 * part * n_cols, transcendentals=0
    )
    scratch = [
        pltpu.VMEM((n_parts, part, n_cols), bf16),
        pltpu.VMEM((n_parts, part, width), bf16),
        pltpu.SemaphoreType.DMA((2 * n_parts,)),
    ]
    args = list(weights) + list(rows)
    return call(kernel, out, args, far=range(2 * n_parts), scratch=scratch, vmem=20, cost=cost)


def structure_parts(blocks, own, got, coef, local):
    feats = blocks.shape[2]

    def kernel(scale, blocks_ref, own_ref, got_ref, out, held, sems):
        loads = copies(
            [(blocks_ref.at[z, pl.ds(0, local)], held.at[z]) for z in range(NZ)], sems
        )
        for r in range(NR):
            for m in range(NM):
                loads[r * NM + m].wait()
            rows = slice(r * local, (r + 1) * local)
            wide = [held[r * NM + m].astype(f32) for m in range(NM)]
            grads = scale[0] * (own_ref[rows] + got_ref[rows].astype(f32))
            grads = [grads[:, m * feats : (m + 1) * feats] for m in range(NM)]
            squares = sum(jnp.sum(w * w, 1, keepdims=True) for w in wide)
            inverse = 1.0 / jnp.sqrt(squares + epsilon)
            dots = sum(jnp.sum(w * g, 1, keepdims=True) for w, g in zip(wide, grads))
            dots = dots * inverse * inverse
            for m in range(NM):
                start = (r * NM + m) * local
                done = (grads[m] - wide[m] * dots) * inverse
                out[start : start + local, :] = done.astype(bf16)

    out = shaped((NZ * local, feats), bf16)
    scratch = [pltpu.VMEM((NZ, local, feats), bf16), pltpu.SemaphoreType.DMA((NZ,))]
    args = [jnp.reshape(coef, (1,)), blocks, own, got]
    return call(kernel, out, args, 1, (1,), (), scratch, 16)


def to_owners(blocks, c_at, rep_at, meanwhile):
    half = blocks.shape[0] // NC
    pairs = [
        (dp_index(y, x, k) * NR + 1 - k, dp_index(y, x, k) * NR + k)
        for y in range(NY)
        for x in range(NX)
        for k in range(NC)
    ]
    got = tied(lax.ppermute(blocks.astype(bf16), ("dp", "rep"), pairs), meanwhile)
    total = blocks + got.astype(f32)
    first = c_at == 0
    own = jnp.where(first, total[:half], total[half:])
    got = from_core(jnp.where(first, total[half:], total[:half]))
    return jnp.where(c_at == rep_at, own, got)


def body(emb_a, emb_b, keep, loss_scale, hidden_a, proj_a):
    dp_at = lax.axis_index("dp")
    mp_at = lax.axis_index("mp")
    rep_at = lax.axis_index("rep")
    y_at, x_at, c_at = dp_at // (NX * NC), dp_at // NC % NX, dp_at % NC
    local = emb_a.shape[0]
    piece = local // NM

    z_at = rep_at * NM + mp_at
    ring = ("rep", "mp")

    own_block = structure_block(keep, emb_b, proj_a)
    gathered = lax.all_gather(own_block, ring)
    emb_a = tied(emb_a, own_block)
    parts = [block_at(emb_a, mp_at, 0, NM)]
    for k in (1, 2, 3):
        parts.append(from_mp(block_at(emb_a, mp_at + NM - k, 0, NM), k))
    wide_a = turned(parts, NM - mp_at, 1).astype(f32)
    _, units_a = normalize(wide_a)
    marker = jnp.where(jnp.arange(wide_a.shape[-1]) == 0, 2.0, 0.0).astype(bf16)[None, :]
    marked_a = jnp.where(block_at(keep, mp_at, 0, NM)[:, None] > 0, units_a, marker)
    chip_piece = jnp.concatenate(
        [block_at(marked_a, c_at, 0, NC), from_core(block_at(marked_a, 1 - c_at, 0, NC))], 0
    )
    line = line_gather(chip_piece)
    rows_u = [line] + [from_second(line, d) for d in OFFSETS[1:]]
    cols_own, proj_ring = structure_units(tied(gathered, rows_u), local)
    columns = [[y * NX * NC + i for y in range(NY)] for i in range(NX * NC)]
    rows_of_chips = [[y * NX * NC + i for i in range(NX * NC)] for y in range(NY)]
    proj_column = lax.all_gather(proj_ring, "dp", axis_index_groups=columns)
    cols_u = [cols_own, from_core(cols_own)]
    row_lse, col_info, kept_cols = score_sums(rows_u, cols_u)
    row_lse, col_info = row_lse.reshape(-1), col_info.reshape(-1)
    for axis, d, col_step in ((1, 1, 1), (1, 2, 2), (0, 1, 4), (0, 2, 0)):
        row_other = (from_first if axis else from_second)(row_lse, d)
        col_other = from_z(col_info, col_step) if col_step else cols_swapped(from_core(col_info))
        row_lse = log_add(row_lse, rows_aligned(row_other, axis, d))
        col_info = log_add(col_info, col_other)
    count = jnp.exp(col_info[-1])
    coef = loss_scale[0] * logit_scale / (2.0 * count)

    half = piece // NC
    start = z_at * piece + c_at * half
    weights, row_grads = [None] * 4, [None] * 4
    size = rows_u[0].shape[0]
    for t in (2, 1, 3, 0):
        weights[t], row_grads[t] = weights_and_row_grads(
            rows_u[t],
            kept_cols,
            row_lse[None, t * size : (t + 1) * size],
            col_info[None],
            cols_u,
            start,
            half if t == 0 else 0,
        )
    got = line_received(row_grads)
    col_own, col_other = col_products(weights, rows_u)
    got = tied(got, col_own)
    first_a, *parts_a = line_added(row_grads[0], got)
    proj_column = tied(proj_column, first_a)
    proj_rows = block_copied(proj_column, mp_at)
    proj_rows = lax.all_gather(proj_rows, "dp", axis=0, tiled=True, axis_index_groups=rows_of_chips)
    col_got = from_core(tied(col_other, first_a))
    parts_a = tied(parts_a, col_own)
    got = piece_received(parts_a)
    half_own, half_other = halves_added(first_a, got)
    grad_a = spectrum_finished(half_own, from_core(half_other), wide_a, coef, c_at)

    pieces = [grad_a] + [from_mp(grad_a, -k) for k in (1, 2, 3)]
    partial_b = structure_parts(gathered, tied(col_own, grad_a), col_got, coef, local)
    grad_emb_b = lax.psum_scatter(partial_b, ring, scatter_dimension=0, tiled=True)
    pieces = tied(pieces, partial_b)
    hidden_t = hidden_prepared(hidden_a, y_at, x_at, c_at, mp_at)
    proj_own, proj_other = proj_products(hidden_t.reshape(NR, -1, local), pieces, mp_at)
    chip_parts = quarters_added(proj_own, from_core(proj_other))
    got = line_received(chip_parts)
    grad_hidden = hidden_gradient(pieces, tied(proj_rows, chip_parts), mp_at)
    first_p, *parts_p = line_added(chip_parts[0], got)
    owned = sum([g.astype(f32) for g in piece_received(parts_p)], first_p)
    grad_proj = to_owners(owned, c_at, rep_at, (grad_hidden, grad_emb_b))
    return (grad_hidden, grad_proj, grad_emb_b)


def solution(mesh):
    return jax.shard_map(
        body,
        mesh=mesh,
        in_specs=(
            P(("dp", "rep"), "mp"),
            P(("dp", "rep"), "mp"),
            P(("dp", "rep")),
            P(),
            P(("dp", "rep"), None),
            P(("dp", "rep"), "mp"),
        ),
        out_specs=(P(("dp", "rep"), "mp"), P(("dp", "rep"), "mp"), P(("dp", "rep"), "mp")),
        check_vma=False,
    )
```

```python
import jax
import jax.numpy as jnp
from jax import lax
from jax.experimental import pallas as pl
from jax.experimental.pallas import tpu as pltpu
from jax.sharding import PartitionSpec as P

logit_scale = 100.0
masked_score = -1e30
epsilon = 1e-06
NX, NY, NC = 4, 4, 2
NM, NR = 4, 2
NZ = NM * NR
bf16 = jnp.bfloat16
f32 = jnp.float32


def dp_index(y, x, c):
    return ((y % NY) * NX + x % NX) * NC + c % NC


def dp_perm(to):
    return [
        (dp_index(y, x, c), dp_index(*to(y, x, c)))
        for y in range(NY)
        for x in range(NX)
        for c in range(NC)
    ]


def z_index(z):
    z = z % NZ
    return (z % NM) * NR + z // NM


def shift_perm(d, swapped):
    return dp_perm(
        lambda y, x, c: (y, x - d, c) if (c == 0) != swapped else (y - d, x, c)
    )


def from_first(v, d):
    return lax.ppermute(v, "dp", shift_perm(d, False))


def from_second(v, d):
    return lax.ppermute(v, "dp", shift_perm(d, True))


def from_core(v):
    return lax.ppermute(v, "dp", dp_perm(lambda y, x, c: (y, x, 1 - c)))


def from_z(v, d):
    return lax.ppermute(v, ("mp", "rep"), [(z_index(z), z_index(z - d)) for z in range(NZ)])


def from_mp(v, d):
    return lax.ppermute(v, "mp", [(m, (m - d) % NM) for m in range(NM)])


OFFSETS = (0, 1, 2, -1)


def tied(value, *others):
    return lax.optimization_barrier((value, others))[0]


def line_gather(piece):
    return jnp.concatenate([piece] + [from_first(piece, d) for d in OFFSETS[1:]], 0)


def line_received(blocks):
    return [from_second(blocks[i], -OFFSETS[i]) for i in (1, 2, 3)]


def line_added(own, got):
    size = own.shape[0] // 4

    def kernel(own_ref, got_1, got_2, got_3, first, *others):
        for i, out in enumerate((first,) + others):
            rows = slice(i * size, (i + 1) * size)
            total = own_ref[rows, :].astype(f32)
            for g in (got_1, got_2, got_3):
                total = total + g[rows, :].astype(f32)
            out[...] = total.astype(out.dtype)

    shape = (size, own.shape[1])
    return call(kernel, (shaped(shape, f32),) + (shaped(shape, bf16),) * 3, [own] + got)


def piece_received(parts):
    return [from_first(parts[i - 1], -OFFSETS[i]) for i in (1, 2, 3)]


def halves_added(own, got):
    half = own.shape[0] // NC

    def kernel(own_ref, got_1, got_2, got_3, *outs):
        for i, out in enumerate(outs):
            rows = slice(i * half, (i + 1) * half)
            total = own_ref[rows, :]
            for g in (got_1, got_2, got_3):
                total = total + g[rows, :].astype(f32)
            out[...] = total

    return call(kernel, (shaped((half, own.shape[1]), f32),) * NC, [own] + got)


def spectrum_finished(own, got, wide, coef, c_at):
    half = own.shape[0]

    def kernel(scale, at, own_ref, got_ref, wide_ref, out):
        first = at[0] == 0
        for i in range(NC):
            rows = slice(i * half, (i + 1) * half)
            a, b = (own_ref, got_ref) if i == 0 else (got_ref, own_ref)
            grads = scale[0] * jnp.where(first, a[...], b[...])
            values = wide_ref[rows, :]
            inverse = 1.0 / jnp.sqrt(jnp.sum(values * values, 1, keepdims=True) + epsilon)
            unit = values * inverse
            dots = jnp.sum(unit * grads, 1, keepdims=True)
            out[rows, :] = ((grads - unit * dots) * inverse).astype(bf16)

    at = jnp.reshape(c_at, (1,)).astype(jnp.int32)
    args = [jnp.reshape(coef, (1,)), at, own, got, wide]
    return call(kernel, shaped(wide.shape, bf16), args, 2)


def proj_products(hidden, pieces, mp_at):
    _, n_rows, _ = hidden.shape
    feats = pieces[0].shape[1] // NM
    step = 512

    def kernel(at, hidden_ref, *refs):
        ins, (own, other) = refs[:NM], refs[NM:]
        cols = pl.ds(pl.multiple_of(at[0] * feats, feats), feats)
        mine = jnp.concatenate([p[:, cols] for p in ins], 0)
        for i, out in enumerate((own, other)):
            for j in range(0, n_rows, step):
                g = jnp.dot(hidden_ref[i, j : j + step], mine, preferred_element_type=f32)
                out[j : j + step, :] = g.astype(out.dtype)

    out = (shaped((n_rows, feats), f32), shaped((n_rows, feats), bf16))
    at = jnp.reshape(mp_at, (1,)).astype(jnp.int32)
    return call(kernel, out, [at, hidden] + list(pieces), 1)


def quarters_added(own, got):
    size = own.shape[0] // 4

    def kernel(own_ref, got_ref, *outs):
        for i, out in enumerate(outs):
            rows = slice(i * size, (i + 1) * size)
            out[...] = (own_ref[rows, :] + got_ref[rows, :].astype(f32)).astype(bf16)

    return call(kernel, (shaped((size, own.shape[1]), bf16),) * 4, [own, got])


def hidden_gradient(pieces, proj, mp_at):
    rows, width = pieces[0].shape

    def kernel(at, proj_ref, *refs):
        ins, out = refs[:NM], refs[NM]
        wide = jnp.concatenate([p[...] for p in ins], 0)
        g = lax.dot_general(
            wide, proj_ref[...], (((1,), (1,)), ((), ())), preferred_element_type=f32
        ).astype(bf16)
        for k in range(NM):
            place = lax.rem(at[0] + NM - k, NM) * rows
            out[pl.ds(pl.multiple_of(place, rows), rows), :] = g[k * rows : (k + 1) * rows]

    out = shaped((NM * rows, proj.shape[0]), bf16)
    at = jnp.reshape(mp_at, (1,)).astype(jnp.int32)
    cost = pl.CostEstimate(
        flops=2 * NM * rows * width * proj.shape[0], bytes_accessed=2 * proj.size, transcendentals=0
    )
    return call(kernel, out, [at, proj] + list(pieces), 1, cost=cost)


def turned(blocks, shift, axis):
    n = len(blocks)
    size = blocks[0].shape[axis]
    doubled = jnp.concatenate(list(blocks) + list(blocks)[:-1], axis)
    return lax.dynamic_slice_in_dim(doubled, shift % n * size, n * size, axis)


def block_at(v, index, axis, n):
    size = v.shape[axis] // n
    return lax.dynamic_slice_in_dim(v, index % n * size, size, axis)


def rows_aligned(v, axis, d):
    return jnp.roll(v.reshape(4, 4, -1), d, axis).reshape(v.shape)


def cols_swapped(v):
    n = 128 * (v.shape[0] // 128 - 1) // 2
    return jnp.concatenate([v[n : 2 * n], v[:n], v[2 * n :]])


def log_add(a, b):
    return jnp.maximum(a, b) + jnp.log1p(jnp.exp(-jnp.abs(a - b)))


def normalize(wide):
    norms = jnp.sqrt(jnp.sum(wide * wide, axis=-1) + epsilon)
    return norms, (wide / norms[..., None]).astype(bf16)


def hidden_prepared(hidden, y_at, x_at, c_at, mp_at):
    rows, width = hidden.shape
    wide = width // (NX * NY * NC)
    half = wide // NR

    def kernel(at, hidden_ref, out_ref, turned_ref):
        piece = rows // NM
        core = at[2]
        for k in range(NM):
            source = lax.rem(at[3] + NM - k, NM)
            turned_ref[k * piece : (k + 1) * piece, :] = hidden_ref[
                pl.ds(pl.multiple_of(source * piece, piece), piece), :
            ]
        for i, dy in enumerate(OFFSETS):
            for j, dx in enumerate(OFFSETS):
                y = lax.rem(at[0] + NY + dy, NY)
                x = lax.rem(at[1] + NX + dx, NX)
                for c in range(NC):
                    column = ((y * NX + x) * NC + c) * wide
                    block = turned_ref[:, pl.ds(pl.multiple_of(column, wide), wide)]
                    block = block.astype(f32).T.astype(bf16)
                    for r in range(NR):
                        place = i * NX + j if r == 0 else j * NY + i
                        slot = lax.rem(core + r, NR)
                        out_ref[slot, place, c] = block[r * half : (r + 1) * half]

    return pl.pallas_call(
        kernel,
        out_shape=jax.ShapeDtypeStruct((NR, NX * NY, NC, half, rows), bf16),
        in_specs=[
            pl.BlockSpec(memory_space=pltpu.SMEM),
            pl.BlockSpec(memory_space=pltpu.VMEM),
        ],
        out_specs=pl.BlockSpec(memory_space=pltpu.VMEM),
        scratch_shapes=[pltpu.VMEM((rows, width), bf16)],
        compiler_params=pltpu.CompilerParams(vmem_limit_bytes=24 * 2**20),
    )(jnp.stack([y_at, x_at, c_at, mp_at]).astype(jnp.int32), hidden)


def call(kernel, out_shape, args, smem=0, far=(), far_out=(), scratch=(), vmem=8, cost=None):
    spaces = [pltpu.SMEM if i < smem else pltpu.HBM if i in far else pltpu.VMEM for i in range(len(args))]
    specs = [pl.BlockSpec(memory_space=space) for space in spaces]
    several = isinstance(out_shape, tuple)
    n_out = len(out_shape) if several else 1
    outs = [pl.BlockSpec(memory_space=pltpu.HBM if i in far_out else pltpu.VMEM) for i in range(n_out)]
    return pl.pallas_call(
        kernel,
        out_shape=out_shape,
        in_specs=specs,
        out_specs=tuple(outs) if several else outs[0],
        scratch_shapes=list(scratch),
        cost_estimate=cost,
        compiler_params=pltpu.CompilerParams(vmem_limit_bytes=vmem * 2**20),
    )(*args)


def copies(pairs, sems, first=0):
    started = [
        pltpu.make_async_copy(a, b, sems.at[first + i]) for i, (a, b) in enumerate(pairs)
    ]
    for c in started:
        c.start()
    return started


def shaped(shape, dtype):
    return jax.ShapeDtypeStruct(shape, dtype)


def structure_block(keep, emb, proj):
    local, feats = emb.shape
    extra = proj.shape[0]

    def kernel(keep_ref, emb_ref, proj_ref, out, held, sems):
        loads = copies(
            [(emb_ref, held.at[pl.ds(0, local)]), (proj_ref, held.at[pl.ds(local, extra)])], sems
        )
        kept = jnp.broadcast_to(keep_ref[...].astype(f32), (128, local)).T[:, :1] > 0.5
        loads[0].wait()
        held[:local, :] = jnp.where(kept, held[:local, :].astype(f32), 8.0).astype(bf16)
        loads[1].wait()
        store = copies([(held, out)], sems, 2)[0]
        store.wait()

    scratch = [pltpu.VMEM((local + extra, feats), bf16), pltpu.SemaphoreType.DMA((3,))]
    out = shaped((local + extra, feats), bf16)
    return call(kernel, out, [keep[None], emb, proj], far=(1, 2), far_out=(0,), scratch=scratch)


def structure_units(blocks, local):
    _, height, feats = blocks.shape
    extra = height - local

    def kernel(held, units, proj):
        for r in range(NR):
            rows = slice(r * local, (r + 1) * local)
            wide = [held[r * NM + m, :local].astype(f32) for m in range(NM)]
            squares = sum(jnp.sum(w * w, 1, keepdims=True) for w in wide)
            inverse = 1.0 / jnp.sqrt(squares + epsilon)
            dropped = wide[0][:, :1] > 4.0
            lane = lax.broadcasted_iota(jnp.int32, (local, feats), 1)
            for m in range(NM):
                cols = slice(m * feats, (m + 1) * feats)
                marker = jnp.where(lane == 0, 2.0, 0.0) if m == 0 else jnp.zeros_like(wide[m])
                units[rows, cols] = jnp.where(dropped, marker, wide[m] * inverse).astype(bf16)
                proj[r * extra : (r + 1) * extra, cols] = held[r * NM + m, local:]

    out = (shaped((NR * local, NM * feats), bf16), shaped((NR * extra, NM * feats), bf16))
    return call(kernel, out, [blocks], vmem=10)


def block_copied(blocks, index):
    def kernel(at, blocks_ref, out, sems):
        copies([(blocks_ref.at[at[0]], out)], sems)[0].wait()

    at = jnp.reshape(index, (1,)).astype(jnp.int32)
    scratch = [pltpu.SemaphoreType.DMA((1,))]
    return call(kernel, shaped(blocks.shape[1:], bf16), [at, blocks], 1, (1,), (0,), scratch, 1)


def scores_of(row, cols, kept_cols):
    nt = (((1,), (1,)), ((), ()))
    kept_rows = row[:, :1].astype(f32) < 1.5
    s = [lax.dot_general(row, c[...], nt, preferred_element_type=f32) for c in cols]
    s = logit_scale * jnp.concatenate(s, 1)
    return jnp.where(kept_rows & kept_cols, s, masked_score), kept_rows


def score_sums(rows, cols):
    part, width = rows[0].shape
    n_rows, n_cols = len(rows) * part, sum(c.shape[0] for c in cols)

    def kernel(*refs):
        col_refs, (row_out, col_out, kept_out) = refs[len(rows) :][: len(cols)], refs[-4:-1]
        row_refs, scores = refs[: len(rows)], refs[-1]
        first = (lax.broadcasted_iota(jnp.int32, (16, width), 1) == 0).astype(f32).astype(bf16)
        nt = (((1,), (1,)), ((), ()))
        marks = [lax.dot_general(first, c[...], nt, preferred_element_type=f32) for c in col_refs]
        kept_cols = jnp.concatenate(marks, 1)[:1] < 1.5
        kept_out[...] = kept_cols.astype(f32)
        col_top = None
        count = jnp.zeros((1, 1), f32)
        for t in range(len(rows)):
            s, kept_rows = scores_of(row_refs[t][...], col_refs, kept_cols)
            count = count + jnp.sum(kept_rows.astype(f32), 0, keepdims=True)
            scores[t] = s
            top = jnp.max(s, 1, keepdims=True)
            lse = top + jnp.log(jnp.sum(jnp.exp(s - top), 1, keepdims=True))
            row_out[:, t * part : (t + 1) * part] = jnp.broadcast_to(lse, (part, 128)).T[:1]
            here = jnp.max(s, 0, keepdims=True)
            col_top = here if col_top is None else jnp.maximum(col_top, here)
        total = jnp.zeros_like(col_top)
        for t in range(len(rows)):
            total = total + jnp.sum(jnp.exp(scores[t] - col_top), 0, keepdims=True)
        col_out[:, :n_cols] = col_top + jnp.log(total)
        col_out[:, n_cols:] = jnp.broadcast_to(jnp.log(count), (1, 128))

    out = (shaped((1, n_rows), f32), shaped((1, n_cols + 128), f32), shaped((1, n_cols), f32))
    cost = pl.CostEstimate(
        flops=2 * n_rows * n_cols * width, bytes_accessed=8 * n_rows * n_cols, transcendentals=0
    )
    scratch = [
        pltpu.VMEM((len(rows), part, n_cols), f32),
    ]
    args = list(rows) + list(cols)
    return call(kernel, out, args, scratch=scratch, vmem=16, cost=cost)


def weights_and_row_grads(row_units, kept, row_lse, col_lse, cols, start, half):
    part, width = row_units.shape
    n_cols = kept.shape[1]
    n_core = n_cols // NC
    n_chunks = 2
    chunk = part // n_chunks

    def kernel(at, units_ref, kept_ref, row_ref, col_ref, own, other, weights, grads):
        col = jnp.maximum(col_ref[:, :n_cols], 0.1 * masked_score)
        row = jnp.maximum(row_ref[...], 0.1 * masked_score)
        row = jnp.broadcast_to(row, (128, part)).T[:, :1]
        kept_cols = kept_ref[...] > 0.5
        for i in range(n_chunks):
            rows = slice(i * chunk, (i + 1) * chunk)
            s, _ = scores_of(units_ref[rows, :], (own, other), kept_cols)
            w = jnp.exp(s - row[rows]) + jnp.exp(s - col)
            if i == 0 and half:
                n = NC * half
                r = lax.broadcasted_iota(jnp.int32, (n, n_cols), 0)
                c = lax.broadcasted_iota(jnp.int32, (n, n_cols), 1)
                partner = at[0] + jnp.where(r < half, r, r - half + n_core)
                own_pair = (c == partner) & (s[:n] > 0.1 * masked_score)
                w = jnp.concatenate([w[:n] - jnp.where(own_pair, 2.0, 0.0), w[n:]], 0)
            w = w.astype(bf16)
            weights[rows, :] = w
            g = jnp.dot(w[:, :n_core], own[...], preferred_element_type=f32)
            g = g + jnp.dot(w[:, n_core:], other[...], preferred_element_type=f32)
            grads[rows, :] = g.astype(bf16)

    out = (shaped((part, n_cols), bf16), shaped((part, width), bf16))
    at = jnp.reshape(start, (1,)).astype(jnp.int32)
    cost = pl.CostEstimate(
        flops=4 * part * n_cols * width, bytes_accessed=8 * part * n_cols, transcendentals=0
    )
    args = [at, row_units, kept, row_lse, col_lse] + list(cols)
    return call(kernel, out, args, 1, vmem=10, cost=cost)


def col_products(weights, rows):
    part, width = rows[0].shape
    n_cols = weights[0].shape[1]
    n_parts = len(rows)
    n_core = n_cols // NC
    step = min(256, n_core)

    def kernel(*refs):
        own, other, w, row_refs, sems = refs[2 * n_parts :]
        loads = copies([(refs[t], w.at[t]) for t in range(n_parts)], sems)
        loads += copies([(refs[n_parts + t], row_refs.at[t]) for t in range(n_parts)], sems, n_parts)
        for load in loads:
            load.wait()
        for j in range(n_cols // step):
            total = None
            for t in range(n_parts):
                term = lax.dot_general(
                    w[t, :, j * step : (j + 1) * step],
                    row_refs[t],
                    (((0,), (0,)), ((), ())),
                    preferred_element_type=f32,
                )
                total = term if total is None else total + term
            place = j * step % n_core
            if j * step < n_core:
                own[place : place + step, :] = total
            else:
                other[place : place + step, :] = total.astype(bf16)

    out = (shaped((n_core, width), f32), shaped((n_core, width), bf16))
    cost = pl.CostEstimate(
        flops=2 * n_parts * part * n_cols * width, bytes_accessed=8 * part * n_cols, transcendentals=0
    )
    scratch = [
        pltpu.VMEM((n_parts, part, n_cols), bf16),
        pltpu.VMEM((n_parts, part, width), bf16),
        pltpu.SemaphoreType.DMA((2 * n_parts,)),
    ]
    args = list(weights) + list(rows)
    return call(kernel, out, args, far=range(2 * n_parts), scratch=scratch, vmem=20, cost=cost)


def structure_parts(blocks, own, got, coef, local):
    feats = blocks.shape[2]

    def kernel(scale, blocks_ref, own_ref, got_ref, out, held, sems):
        loads = copies(
            [(blocks_ref.at[z, pl.ds(0, local)], held.at[z]) for z in range(NZ)], sems
        )
        for r in range(NR):
            for m in range(NM):
                loads[r * NM + m].wait()
            rows = slice(r * local, (r + 1) * local)
            wide = [held[r * NM + m].astype(f32) for m in range(NM)]
            grads = scale[0] * (own_ref[rows] + got_ref[rows].astype(f32))
            grads = [grads[:, m * feats : (m + 1) * feats] for m in range(NM)]
            squares = sum(jnp.sum(w * w, 1, keepdims=True) for w in wide)
            inverse = 1.0 / jnp.sqrt(squares + epsilon)
            dots = sum(jnp.sum(w * g, 1, keepdims=True) for w, g in zip(wide, grads))
            dots = dots * inverse * inverse
            for m in range(NM):
                start = (r * NM + m) * local
                done = (grads[m] - wide[m] * dots) * inverse
                out[start : start + local, :] = done.astype(bf16)

    out = shaped((NZ * local, feats), bf16)
    scratch = [pltpu.VMEM((NZ, local, feats), bf16), pltpu.SemaphoreType.DMA((NZ,))]
    args = [jnp.reshape(coef, (1,)), blocks, own, got]
    return call(kernel, out, args, 1, (1,), (), scratch, 16)


def to_owners(blocks, c_at, rep_at, meanwhile, at_last):
    half = blocks.shape[0] // NC
    pairs = [
        (dp_index(y, x, k) * NR + 1 - k, dp_index(y, x, k) * NR + k)
        for y in range(NY)
        for x in range(NX)
        for k in range(NC)
    ]
    got = tied(lax.ppermute(blocks.astype(bf16), ("dp", "rep"), pairs), meanwhile)
    total = blocks + got.astype(f32)
    first = c_at == 0
    own = jnp.where(first, total[:half], total[half:])
    got = tied(from_core(jnp.where(first, total[half:], total[:half])), at_last)
    return jnp.where(c_at == rep_at, own, got)


def body(emb_a, emb_b, keep, loss_scale, hidden_a, proj_a):
    dp_at = lax.axis_index("dp")
    mp_at = lax.axis_index("mp")
    rep_at = lax.axis_index("rep")
    y_at, x_at, c_at = dp_at // (NX * NC), dp_at // NC % NX, dp_at % NC
    local = emb_a.shape[0]
    piece = local // NM

    z_at = rep_at * NM + mp_at
    ring = ("rep", "mp")

    own_block = structure_block(keep, emb_b, proj_a)
    gathered = lax.all_gather(own_block, ring)
    emb_a = tied(emb_a, own_block)
    parts = [block_at(emb_a, mp_at, 0, NM)]
    for k in (1, 2, 3):
        parts.append(from_mp(block_at(emb_a, mp_at + NM - k, 0, NM), k))
    wide_a = turned(parts, NM - mp_at, 1).astype(f32)
    _, units_a = normalize(wide_a)
    marker = jnp.where(jnp.arange(wide_a.shape[-1]) == 0, 2.0, 0.0).astype(bf16)[None, :]
    marked_a = jnp.where(block_at(keep, mp_at, 0, NM)[:, None] > 0, units_a, marker)
    chip_piece = jnp.concatenate(
        [block_at(marked_a, c_at, 0, NC), from_core(block_at(marked_a, 1 - c_at, 0, NC))], 0
    )
    line = line_gather(chip_piece)
    rows_u = [line] + [from_second(line, d) for d in OFFSETS[1:]]
    cols_own, proj_ring = structure_units(tied(gathered, rows_u), local)
    columns = [[y * NX * NC + i for y in range(NY)] for i in range(NX * NC)]
    rows_of_chips = [[y * NX * NC + i for i in range(NX * NC)] for y in range(NY)]
    proj_column = lax.all_gather(proj_ring, "dp", axis_index_groups=columns)
    cols_u = [cols_own, from_core(cols_own)]
    row_lse, col_info, kept_cols = score_sums(rows_u, cols_u)
    row_lse, col_info = row_lse.reshape(-1), col_info.reshape(-1)
    for axis, d, col_step in ((1, 1, 1), (1, 2, 2), (0, 1, 4), (0, 2, 0)):
        row_other = (from_first if axis else from_second)(row_lse, d)
        col_other = from_z(col_info, col_step) if col_step else cols_swapped(from_core(col_info))
        row_lse = log_add(row_lse, rows_aligned(row_other, axis, d))
        col_info = log_add(col_info, col_other)
    count = jnp.exp(col_info[-1])
    coef = loss_scale[0] * logit_scale / (2.0 * count)

    half = piece // NC
    start = z_at * piece + c_at * half
    weights, row_grads = [None] * 4, [None] * 4
    size = rows_u[0].shape[0]
    for t in (2, 1, 3, 0):
        weights[t], row_grads[t] = weights_and_row_grads(
            rows_u[t],
            kept_cols,
            row_lse[None, t * size : (t + 1) * size],
            col_info[None],
            cols_u,
            start,
            half if t == 0 else 0,
        )
    got = line_received(row_grads)
    col_own, col_other = col_products(weights, rows_u)
    got = tied(got, col_own)
    first_a, *parts_a = line_added(row_grads[0], got)
    proj_column = tied(proj_column, first_a)
    proj_rows = block_copied(proj_column, mp_at)
    proj_rows = lax.all_gather(proj_rows, "dp", axis=0, tiled=True, axis_index_groups=rows_of_chips)
    col_got = from_core(tied(col_other, first_a))
    parts_a = tied(parts_a, col_own)
    got = piece_received(parts_a)
    half_own, half_other = halves_added(first_a, got)
    grad_a = spectrum_finished(half_own, from_core(half_other), wide_a, coef, c_at)

    pieces = [grad_a] + [from_mp(grad_a, -k) for k in (1, 2, 3)]
    partial_b = structure_parts(gathered, tied(col_own, grad_a), col_got, coef, local)
    grad_emb_b = lax.psum_scatter(partial_b, ring, scatter_dimension=0, tiled=True)
    pieces = tied(pieces, partial_b)
    hidden_t = hidden_prepared(hidden_a, y_at, x_at, c_at, mp_at)
    proj_own, proj_other = proj_products(hidden_t.reshape(NR, -1, local), pieces, mp_at)
    chip_parts = quarters_added(proj_own, from_core(proj_other))
    got = line_received(chip_parts)
    grad_hidden = hidden_gradient(pieces, tied(proj_rows, chip_parts), mp_at)
    first_p, *parts_p = line_added(chip_parts[0], got)
    owned = sum([g.astype(f32) for g in piece_received(parts_p)], first_p)
    grad_proj = to_owners(owned, c_at, rep_at, grad_hidden, grad_emb_b)
    return (grad_hidden, grad_proj, grad_emb_b)


def solution(mesh):
    return jax.shard_map(
        body,
        mesh=mesh,
        in_specs=(
            P(("dp", "rep"), "mp"),
            P(("dp", "rep"), "mp"),
            P(("dp", "rep")),
            P(),
            P(("dp", "rep"), None),
            P(("dp", "rep"), "mp"),
        ),
        out_specs=(P(("dp", "rep"), "mp"), P(("dp", "rep"), "mp"), P(("dp", "rep"), "mp")),
        check_vma=False,
    )
```
